32 devices in a mesh: lev: 4 (over y, core), tile: 8 (over z, x).
Axes of the slice: x: 2, y: 2, z: 4, core: 2. Of those that a mesh axis runs over, the one named last changes fastest.
Arguments:
- levels: bfloat16 [16, 24, 96, 512], P('lev', None, 'tile'), may hold values from -6 to 6
- level_mask: int32 [16], P('lev'), may hold values from 0 to 1, as said below
- w_key: bfloat16 [512, 512], replicated, may hold values from -0.25 to 0.25
- w_value: bfloat16 [512, 512], replicated, may hold values from -0.25 to 0.25
- latent_query: bfloat16 [4, 512], replicated, may hold values from -52 to 52
- w_agg_out: bfloat16 [512, 512], replicated, may hold values from -0.25 to 0.25
- gain_attn: float32 [512], replicated, may hold values from 0.1 to 1.9
- w_qkv: bfloat16 [512, 1536], replicated, may hold values from -3 to 3
- w_proj: bfloat16 [512, 512], replicated, may hold values from -0.25 to 0.25
- gain_mlp: float32 [512], replicated, may hold values from 0.1 to 1.9
- w_up: bfloat16 [512, 2048], replicated, may hold values from -0.25 to 0.25
- w_down: bfloat16 [2048, 512], replicated, may hold values from -0.125 to 0.125
- cotangent: bfloat16 [4, 24, 96, 512], P(None, None, 'tile'), may hold values from -6 to 6
Outputs:
- encoded: bfloat16 [4, 24, 96, 512], P(None, None, 'tile')
- grad_up: float32 [512, 2048], P('lev', 'tile')
- grad_down_t: float32 [512, 2048], P('lev', 'tile')
The draws below stay inside these ranges and needn't reach their ends.
Inputs may be any that keep to these rules, and one draw needn't show every extreme that they name: `level_mask`: exactly 13 of the entries are 1, the others 0.
All inputs are finite; a program needn't handle non-finite values.
Results may differ from the reference program's by a relative error of at most 0.03.
The reference program's roundings to bfloat16 on the way count: a program that leaves them out, or rounds other values in their place, can miss the bound.
Values may be sent and summed in bfloat16 or wider, within the bound.
No kernel may reach another device: no remote copies, remote signals or barrier semaphores. Data moves between devices by JAX's collectives and lax.ppermute only.
A program may use at most 128 MiB of HBM per device.

```python
import math
import jax
import jax.numpy as jnp
from jax import lax

D = 512
HEADS = 8
FF = 2048
LEVELS = 16
REAL_LEV = 13
LATENT = 4
WL = 2
WA = 6
WO = 12
TLAT = 24
LON = 96


def draw_levels(key, part):
    key = jax.random.fold_in(key, 14)
    first = jax.random.fold_in(key, 0)
    base = jnp.clip(jax.random.normal(first, (LEVELS, TLAT, LON, D), jnp.float32), -6.0, 6.0)
    return base.astype(jnp.bfloat16)


def draw_level_mask(key, part):
    key = jax.random.fold_in(key, 11)
    order = jax.random.permutation(key, LEVELS)
    return (order < REAL_LEV).astype(jnp.int32)


def draw_latent_query(key, part):
    key = jax.random.fold_in(key, 12)
    first = jax.random.fold_in(key, 0)
    base = jnp.clip(jax.random.normal(first, (LATENT, D), jnp.float32), -4.0, 4.0)
    return base.astype(jnp.bfloat16)


def draw_w_qkv(key, part):
    key = jax.random.fold_in(key, 13)
    first = jax.random.fold_in(key, 0)
    base = jnp.clip(jax.random.normal(first, (D, 3 * D), jnp.float32), -4.0, 4.0) / math.sqrt(D)
    return base.astype(jnp.bfloat16)


def steps_of(own_key, shape, shards, low, high):
    level, own = 1.0, jax.random.fold_in(own_key, 6)
    for position, shards_of in shards:
        steps = jnp.exp(jax.random.uniform(jax.random.fold_in(own, position), (shards_of,), jnp.float32, low / len(shards), high / len(shards)))
        level = level * jnp.repeat(steps, shape[position] // shards_of).reshape([-1 if axis == position else 1 for axis in range(len(shape))])
    return level


def gaussian(stream_key, shape, scale, reach, cuts=(), held_as=jnp.bfloat16):
    entries = scale * jax.random.normal(stream_key, shape, jnp.float32)
    if cuts:
        entries = entries * steps_of(stream_key, shape, cuts, -0.22, 0.18)
    return jnp.clip(entries, -reach, reach).astype(held_as)


def setup_inputs(seed: int = 0) -> dict:
    seeds = jax.random.split(jax.random.key(seed), 14)
    levels = draw_levels(jax.random.fold_in(seeds[13], 71), 0)
    level_mask = draw_level_mask(jax.random.fold_in(seeds[13], 71), 0)
    w_key = gaussian(seeds[2], (D, D), D ** -0.5, 0.25)
    w_value = gaussian(seeds[3], (D, D), D ** -0.5, 0.25)
    latent_query = draw_latent_query(jax.random.fold_in(seeds[13], 71), 0)
    w_agg_out = gaussian(seeds[5], (D, D), D ** -0.5, 0.25)
    gain_attn = jnp.clip(1.0 + 0.18 * jax.random.normal(seeds[6], (D,), jnp.float32), 0.1, 1.9)
    w_qkv = draw_w_qkv(jax.random.fold_in(seeds[13], 71), 0)
    w_proj = gaussian(seeds[8], (D, D), D ** -0.5, 0.25)
    gain_mlp = jnp.clip(1.0 + 0.18 * jax.random.normal(seeds[9], (D,), jnp.float32), 0.1, 1.9)
    w_up = gaussian(seeds[10], (D, FF), D ** -0.5, 0.25)
    w_down = gaussian(seeds[11], (FF, D), FF ** -0.5, 0.125)
    cotangent = gaussian(seeds[12], (LATENT, TLAT, LON, D), 1.0, 6.0, ((2, 8),))
    return dict(levels=levels, level_mask=level_mask, w_key=w_key, w_value=w_value, latent_query=latent_query, w_agg_out=w_agg_out, gain_attn=gain_attn, w_qkv=w_qkv, w_proj=w_proj, gain_mlp=gain_mlp, w_up=w_up, w_down=w_down, cotangent=cotangent)


def layer_norm(rows, gain):
    rows = rows.astype(jnp.float32)
    mean = lax.optimization_barrier(jnp.mean(rows, -1, keepdims=True))
    centred = rows - mean
    spread = lax.optimization_barrier(jnp.mean(centred * centred, -1, keepdims=True))
    return (centred * lax.rsqrt(spread + 1e-05) * gain.astype(jnp.float32)).astype(jnp.bfloat16)

def to_windows(field):
    latent, lat, lon, width = field.shape
    shaped = field.reshape(latent // WL, WL, lat // WA, WA, lon // WO, WO, width)
    shaped = shaped.transpose(0, 2, 4, 1, 3, 5, 6)
    return shaped.reshape(-1, WL * WA * WO, width)

def from_windows(blocks, latent, lat, lon):
    width = blocks.shape[-1]
    shaped = blocks.reshape(latent // WL, lat // WA, lon // WO, WL, WA, WO, width)
    return shaped.transpose(0, 3, 1, 4, 2, 5, 6).reshape(latent, lat, lon, width)

def region_labels(latent, lat, lon):
    lev_idx = lax.broadcasted_iota(jnp.int32, (latent, lat, lon, 1), 0)
    lat_idx = lax.broadcasted_iota(jnp.int32, (latent, lat, lon, 1), 1)
    lev_region = (lev_idx >= latent - WL).astype(jnp.int32) + (lev_idx >= latent - WL // 2).astype(jnp.int32)
    lat_region = (lat_idx >= lat - WA).astype(jnp.int32) + (lat_idx >= lat - WA // 2).astype(jnp.int32)
    return to_windows(lev_region * 3 + lat_region)[..., 0]

def window_block(blocks, labels, gain_attn, w_qkv, w_proj, gain_mlp, w_up, w_down):
    count, size, width = blocks.shape
    head_size = width // HEADS
    rows = blocks.reshape(-1, width)
    normed = layer_norm(rows, gain_attn)
    qkv = jnp.dot(normed, w_qkv, preferred_element_type=jnp.float32).astype(jnp.bfloat16)
    qkv = qkv.reshape(count, size, 3, HEADS, head_size)
    query, key, value = (qkv[:, :, 0], qkv[:, :, 1], qkv[:, :, 2])
    scores = jnp.einsum('wqhe,wkhe->whqk', query.astype(jnp.float32), key.astype(jnp.float32)) * head_size ** (-0.5)
    allowed = labels[:, None, :, None] == labels[:, None, None, :]
    scores = jnp.where(allowed, scores, -1e+30)
    weights = jnp.exp(scores - lax.optimization_barrier(jnp.max(scores, -1, keepdims=True)))
    probs = (weights / lax.optimization_barrier(jnp.sum(weights, -1, keepdims=True))).astype(jnp.bfloat16)
    mixed = jnp.einsum('whqk,wkhe->wqhe', probs.astype(jnp.float32), value.astype(jnp.float32))
    mixed = mixed.astype(jnp.bfloat16).reshape(-1, width)
    resid = (rows.astype(jnp.float32) + jnp.dot(mixed, w_proj, preferred_element_type=jnp.float32)).astype(jnp.bfloat16)
    normed2 = layer_norm(resid, gain_mlp)
    inner = jnp.dot(normed2, w_up, preferred_element_type=jnp.float32)
    active = jax.nn.gelu(inner).astype(jnp.bfloat16)
    output = (resid.astype(jnp.float32) + jnp.dot(active, w_down, preferred_element_type=jnp.float32)).astype(jnp.bfloat16)
    return (output, normed2, inner, active)

def reference(levels, level_mask, w_key, w_value, latent_query, w_agg_out, gain_attn, w_qkv, w_proj, gain_mlp, w_up, w_down, cotangent):
    count, lat, lon, width = levels.shape
    head_size = width // HEADS
    flat = levels.reshape(-1, width)
    keys = jnp.dot(flat, w_key, preferred_element_type=jnp.float32).astype(jnp.bfloat16)
    keys = keys.reshape(count, lat, lon, HEADS, head_size)
    values = jnp.dot(flat, w_value, preferred_element_type=jnp.float32).astype(jnp.bfloat16)
    values = values.reshape(count, lat, lon, HEADS, head_size)
    query = latent_query.astype(jnp.float32).reshape(LATENT, HEADS, head_size)
    scores = jnp.einsum('lhe,jaohe->ljaoh', query, keys.astype(jnp.float32)) * head_size ** (-0.5)
    live = (level_mask > 0)[None, :, None, None, None]
    scores = jnp.where(live, scores, -1e+30)
    top = lax.optimization_barrier(jnp.max(scores, 1, keepdims=True))
    weights = jnp.exp(scores - top) * live.astype(jnp.float32)
    total = lax.optimization_barrier(jnp.sum(weights, 1))
    summed = jnp.einsum('ljaoh,jaohe->laohe', weights, values.astype(jnp.float32))
    pooled = (summed / total[..., None]).astype(jnp.bfloat16).reshape(-1, width)
    latent = jnp.dot(pooled, w_agg_out, preferred_element_type=jnp.float32).astype(jnp.bfloat16)
    latent = latent.reshape(LATENT, lat, lon, width)
    rolled = jnp.roll(latent, (-(WL // 2), -(WA // 2), -(WO // 2)), (0, 1, 2))
    blocks = to_windows(rolled)
    labels = region_labels(LATENT, lat, lon)
    output, normed2, inner, active = window_block(blocks, labels, gain_attn, w_qkv, w_proj, gain_mlp, w_up, w_down)
    encoded = from_windows(output.reshape(blocks.shape), LATENT, lat, lon)
    encoded = jnp.roll(encoded, (WL // 2, WA // 2, WO // 2), (0, 1, 2))
    rolled_cot = jnp.roll(cotangent, (-(WL // 2), -(WA // 2), -(WO // 2)), (0, 1, 2))
    cot_rows = to_windows(rolled_cot).reshape(-1, width)
    back = jnp.dot(cot_rows, w_down.T, preferred_element_type=jnp.float32)
    pullback = jax.vjp(jax.nn.gelu, inner)[1]
    dinner = pullback(back)[0].astype(jnp.bfloat16)
    grad_up = jnp.dot(normed2.T, dinner, preferred_element_type=jnp.float32)
    grad_down_t = jnp.dot(cot_rows.T, active, preferred_element_type=jnp.float32)
    return (encoded, grad_up, grad_down_t)
```

```python
import functools

import jax
import jax.numpy as jnp
from jax import lax
from jax.experimental import pallas as pl
from jax.experimental.pallas import tpu as pltpu
from jax.sharding import PartitionSpec as P

HEADS = 8
LATENT = 4
WL = 2
WA = 6
WO = 12
HALF = WO // 2
PIECE = WA * HALF
MARK = 2.0**40
F32 = jnp.float32
BF16 = jnp.bfloat16
MIB = 1 << 20


def dot(a, b, contract=((1,), (0,))):
    return lax.dot_general(a, b, (contract, ((), ())), preferred_element_type=F32)


def call(body, outs, scratch=(), smem_first=0, vmem=40, flops=0, moved=0, n_in=1, smem_last=0):
    ins = [pl.BlockSpec(memory_space=pltpu.SMEM)] * smem_first
    ins += [pl.BlockSpec(memory_space=pltpu.VMEM)] * (n_in - smem_first)
    return pl.pallas_call(
        body,
        out_shape=[jax.ShapeDtypeStruct(shape, dtype) for shape, dtype in outs],
        in_specs=ins,
        out_specs=[pl.BlockSpec(memory_space=pltpu.VMEM)] * len(outs),
        scratch_shapes=list(scratch),
        compiler_params=pltpu.CompilerParams(vmem_limit_bytes=vmem * MIB),
        cost_estimate=pl.CostEstimate(flops=flops, bytes_accessed=moved, transcendentals=0),
    )


def layer_norm(rows, gain):
    mean = jnp.mean(rows, -1, keepdims=True)
    centred = rows - mean
    spread = jnp.mean(centred * centred, -1, keepdims=True)
    return (centred * lax.rsqrt(spread + 1e-05) * gain).astype(BF16)


def gelu_parts(x):
    square = x * x
    t = jnp.tanh(x * (0.7978845608028654 + 0.7978845608028654 * 0.044715 * square))
    return square, t


def pack_levels_body(lev_count, mask_ref, lev_ref, *refs):
    outs, (east, west) = refs[: 2 * lev_count], refs[2 * lev_count :]
    count, lat = lev_ref.shape[0], lev_ref.shape[1]
    me = lax.axis_index("lev")
    for d in range(lev_count):
        other = me ^ d
        for j in range(count):
            live = mask_ref[j] > 0
            for a in range(WA):
                row = lax.rem(other * WA + WA // 2 + a, lat)
                cells = jnp.where(live, lev_ref[j, row].astype(F32), MARK)
                at = pl.ds(j * PIECE + a * HALF, HALF)
                east[at] = cells[HALF:]
                west[at] = cells[:HALF]
        outs[d][...] = east[...].astype(BF16)
        outs[lev_count + d][...] = west[...].astype(BF16)


def pack_cot_body(cot_ref, east_ref, west_ref, east, west):
    lat = cot_ref.shape[1]
    me = lax.axis_index("lev")
    for slot in range(2):
        other = me ^ (2 * slot)
        for l in range(LATENT):
            for a in range(WA):
                row = lax.rem(other * WA + WA // 2 + a, lat)
                cells = cot_ref[(l + WL // 2) % LATENT, row].astype(F32)
                at = pl.ds((slot * LATENT + l) * PIECE + a * HALF, HALF)
                east[at] = cells[HALF:]
                west[at] = cells[:HALF]
    east_ref[...] = east[...].astype(BF16)
    west_ref[...] = west[...].astype(BF16)


def aggregate(chunks, keep, query, w_key, w_value, w_agg_out, pool):
    width = w_key.shape[0]
    head_size = width // HEADS
    pairs = 2 * PIECE
    owner = lax.broadcasted_iota(jnp.int32, (HEADS, width), 1) // head_size
    table = (owner == lax.broadcasted_iota(jnp.int32, (HEADS, width), 0)).astype(F32)
    block_query = jnp.concatenate([table * query[l : l + 1].astype(F32) for l in range(LATENT)], 0)
    block_query = block_query.astype(BF16)
    lanes = LATENT * HEADS
    for h in range(2):
        rows = jnp.concatenate([ref[...] for ref in chunks[h]], 0)
        blocks = rows.shape[0] // pairs
        keys = dot(rows, w_key[...]).astype(BF16)
        values = dot(rows, w_value[...]).astype(BF16).astype(F32)
        scores = dot(keys, block_query, ((1,), (1,))) * head_size ** (-0.5)
        live = rows[:, :lanes].astype(F32) < MARK / 2
        scores = jnp.where(live, scores, -1e30)
        parts = [scores[b * pairs : (b + 1) * pairs] for b in range(blocks)]
        top = functools.reduce(jnp.maximum, parts)
        top = jnp.maximum(top, pltpu.roll(top, PIECE, 0))
        weights = [
            jnp.exp(part - top) * live[b * pairs : (b + 1) * pairs].astype(F32)
            for b, part in enumerate(parts)
        ]
        total = functools.reduce(jnp.add, weights)
        total = total + pltpu.roll(total, PIECE, 0)
        inverse = 1.0 / total
        weights = jnp.concatenate([w * inverse for w in weights], 0)
        high = weights.astype(BF16)
        low = (weights - high.astype(F32)).astype(BF16)
        step = 256
        per = step // head_size
        for l in range(LATENT):
            sums = []
            for n in range(width // step):
                at = l * HEADS + n * per
                head = lax.broadcasted_iota(jnp.int32, (lanes, step), 1) // head_size + at
                pick = (head == lax.broadcasted_iota(jnp.int32, (lanes, step), 0)).astype(BF16)
                spread = dot(high, pick) + dot(low, pick)
                prod = spread * values[:, n * step : (n + 1) * step]
                total_n = functools.reduce(
                    jnp.add, [prod[b * pairs : (b + 1) * pairs] for b in range(blocks)]
                )
                sums.append(total_n + pltpu.roll(total_n, PIECE, 0))
            slot = h * LATENT + (l - WL // 2) % LATENT
            pool[pl.ds(slot * PIECE, PIECE)] = jnp.concatenate(sums, 1)[:PIECE]
    pooled = pool[...].astype(BF16)
    return dot(pooled, w_agg_out[...]).astype(BF16)


def window_attention(lev_count, latent, gain, w_qkv):
    width = latent.shape[1]
    head_size = width // HEADS
    half = LATENT * PIECE
    slab = WL * PIECE
    size = 2 * slab
    normed = layer_norm(latent.astype(F32), gain[...])
    qkv = dot(normed, w_qkv[...])
    last = lax.axis_index("lev") == lev_count - 1
    shape = (2 * size, size)
    q_at = lax.rem(lax.broadcasted_iota(jnp.int32, shape, 0), slab)
    k_at = lax.rem(lax.broadcasted_iota(jnp.int32, shape, 1), slab)
    q_lat = lax.rem(q_at, PIECE) >= PIECE // 2
    k_lat = lax.rem(k_at, PIECE) >= PIECE // 2
    lat_differs = jnp.where(last, (q_lat != k_lat).astype(F32), 0.0)
    lev_differs = ((q_at >= PIECE) != (k_at >= PIECE)).astype(F32)
    lane = lax.broadcasted_iota(jnp.int32, (size, 2 * head_size), 1) < head_size
    mixed = []
    for lb in range(LATENT // WL):
        rows = jnp.concatenate(
            [qkv[lb * slab : (lb + 1) * slab], qkv[half + lb * slab : half + (lb + 1) * slab]], 0
        )
        differs = lat_differs + lev_differs if lb == LATENT // WL - 1 else lat_differs
        allowed = differs == 0.0
        outs = []
        for p in range(HEADS // 2):
            at = 2 * p * head_size
            query = rows[:, at : at + 2 * head_size]
            key = rows[:, width + at : width + at + 2 * head_size].astype(BF16)
            value = rows[:, 2 * width + at : 2 * width + at + 2 * head_size].astype(BF16)
            query = jnp.concatenate([jnp.where(lane, query, 0.0), jnp.where(lane, 0.0, query)], 0)
            scores = dot(query.astype(BF16), key, ((1,), (1,))) * head_size ** (-0.5)
            scores = jnp.where(allowed, scores, -1e30)
            weights = jnp.exp(scores - jnp.max(scores, -1, keepdims=True))
            probs = weights * (1.0 / jnp.sum(weights, -1, keepdims=True))
            out = dot(probs.astype(BF16), value)
            outs.append(jnp.where(lane, out[:size], out[size:]))
        mixed.append(jnp.concatenate(outs, 1))
    mixed = [m[:slab] for m in mixed] + [m[slab:] for m in mixed]
    return jnp.concatenate(mixed, 0).astype(BF16)


def window_body(lev_count, *refs):
    east, west = refs[:lev_count], refs[lev_count : 2 * lev_count]
    (w_key, w_value, query, w_agg_out, gain_attn, w_qkv, w_proj, gain_mlp) = refs[
        2 * lev_count : 2 * lev_count + 8
    ]
    resid_ref, normed2_ref, pool = refs[2 * lev_count + 8 :]
    latent = aggregate((east, west), None, query[...], w_key, w_value, w_agg_out, pool)
    mixed = window_attention(lev_count, latent, gain_attn, w_qkv)
    resid = (latent.astype(F32) + dot(mixed, w_proj[...])).astype(BF16)
    resid_ref[...] = resid
    normed2_ref[...] = layer_norm(resid.astype(F32), gain_mlp[...])


def mlp_body(resid, normed2, w_up, w_down, east_ref, west_ref):
    step = 512
    rows = normed2[...]
    total = resid[...].astype(F32)
    for n in range(w_up.shape[1] // step):
        inner = dot(rows, w_up[:, n * step : (n + 1) * step])
        _, t = gelu_parts(inner)
        active = (inner * (0.5 * (1.0 + t))).astype(BF16)
        total = total + dot(active, w_down[n * step : (n + 1) * step])
    total = total.astype(BF16)
    half = rows.shape[0] // 2
    east_ref[...] = total[:half]
    west_ref[...] = total[half:]


def grad_body(*refs):
    normed2 = refs[:4]
    own_e, own_w, peer_e, peer_w, w_up, w_down, send, keep, acc_up, acc_dn, n_half, c_half = refs[4:]
    me = lax.axis_index("lev")
    half_at = pl.multiple_of((me // 2) * 256, 256)
    piece = own_e.shape[0] // 2
    width = w_up.shape[0]
    cols = w_up.shape[1]
    step = 256
    model = acc_up.shape[0]
    rows, cots = [], []
    for k, (e, w, slot) in enumerate(
        ((own_e, own_w, 0), (own_e, own_w, 1), (peer_e, peer_w, 0), (peer_e, peer_w, 1))
    ):
        n = 2 * piece
        at = pl.ds(k * n, n)
        cot = jnp.concatenate(
            [e[slot * piece : (slot + 1) * piece], w[slot * piece : (slot + 1) * piece]], 0
        )
        rows.append(normed2[k][...])
        cots.append(cot)
        n_half[at] = normed2[k][:, pl.ds(half_at, model)]
        c_half[pl.ds(k * n, piece)] = e[slot * piece : (slot + 1) * piece, pl.ds(half_at, model)]
        c_half[pl.ds(k * n + piece, piece)] = w[
            slot * piece : (slot + 1) * piece, pl.ds(half_at, model)
        ]
    rows = jnp.concatenate(rows, 0)
    cots = jnp.concatenate(cots, 0)
    n_half_v = n_half[...]
    c_half_v = c_half[...]
    for n in range(cols // step):
        at = slice(n * step, (n + 1) * step)
        x = dot(rows, w_up[:, at])
        back = dot(cots, w_down[at], ((1,), (1,)))
        square, t = gelu_parts(x)
        cdf = 0.5 + 0.5 * t
        active = (x * cdf).astype(BF16)
        slope = (0.5 * 0.7978845608028654) + (1.5 * 0.7978845608028654 * 0.044715) * square
        dinner = (back * (cdf + x * ((1.0 - t * t) * slope))).astype(BF16)
        acc_up[:, at] = dot(n_half_v, dinner, ((0,), (0,)))
        acc_dn[:, at] = dot(c_half_v, active, ((0,), (0,)))
    quarter = model // 2
    core = lax.rem(me, 2)
    mine = pl.ds(pl.multiple_of(core * quarter, quarter), quarter)
    other = pl.ds(pl.multiple_of((1 - core) * quarter, quarter), quarter)
    keep[:quarter] = acc_up[mine]
    keep[quarter:] = acc_dn[mine]
    send[:quarter] = acc_up[other].astype(BF16)
    send[quarter:] = acc_dn[other].astype(BF16)


def split_body(groups, keep, recv, own_ref, *refs):
    outs, blocks = refs[:-1], refs[-1]
    cols = keep.shape[1] // groups
    for n in range(groups):
        at = slice(n * cols, (n + 1) * cols)
        blocks[n] = keep[:, at] + recv[:, at].astype(F32)
    me = lax.axis_index("tile") // 2
    own_ref[...] = blocks[me]
    for d in range(1, groups):
        outs[d - 1][...] = blocks[lax.rem(me + d, groups)].astype(BF16)


def total_body(own, *refs):
    received, (up_ref, dn_ref) = refs[:-2], refs[-2:]
    total = own[...]
    for part in received:
        total = total + part[...].astype(F32)
    half = total.shape[0] // 2
    up_ref[...] = total[:half]
    dn_ref[...] = total[half:]


def unpack_body(*refs):
    own, beside, core_own, core_beside, out_ref, scratch = refs
    lat = out_ref.shape[1]
    me = lax.axis_index("lev")
    half = LATENT * PIECE
    for part, d in ((own, 0), (beside, 2), (core_own, 1), (core_beside, 3)):
        scratch[...] = part[...].astype(F32)
        other = me ^ d
        for l in range(LATENT):
            for a in range(WA):
                row = lax.rem(other * WA + WA // 2 + a, lat)
                at = l * PIECE + a * HALF
                cells = jnp.concatenate(
                    [scratch[pl.ds(half + at, HALF)], scratch[pl.ds(at, HALF)]], 0
                )
                out_ref[(l + WL // 2) % LATENT, row] = cells.astype(BF16)


def exchanged(block, lev_step, tile_move):
    levs, tiles = lax.axis_size("lev"), lax.axis_size("tile")
    route = [
        (l * tiles + t, (l ^ lev_step) * tiles + tile_move(t)) for l in range(levs) for t in range(tiles)
    ]
    return lax.ppermute(block, ("lev", "tile"), route)


def per_device(
    levels,
    level_mask,
    w_key,
    w_value,
    latent_query,
    w_agg_out,
    gain_attn,
    w_qkv,
    w_proj,
    gain_mlp,
    w_up,
    w_down,
    cotangent,
):
    levs, tiles = lax.axis_size("lev"), lax.axis_size("tile")
    count, lat, lon, width = levels.shape
    hidden = w_up.shape[1]
    assert lat == levs * WA and lon == WO and levs == 4 and tiles % 2 == 0
    piece = count * PIECE
    rows = LATENT * PIECE
    window = 2 * rows
    groups = tiles // 2
    part = hidden // tiles
    quarter = width // levs

    west = lambda t: (t - 1) % tiles
    east = lambda t: (t + 1) % tiles
    same = lambda t: t
    peer = lambda t: t ^ 1
    next_pair = lambda t: (t - 2) % tiles if t % 2 == 0 else t

    packed = call(
        functools.partial(pack_levels_body, levs),
        [((piece, width), BF16)] * (2 * levs),
        [pltpu.VMEM((piece, width), F32)] * 2,
        smem_first=1,
        n_in=2,
        moved=3 * MIB,
    )(level_mask, levels)
    easts = [packed[0]] + [exchanged(packed[d], d, same) for d in range(1, levs)]
    wests = [exchanged(packed[levs + d], d, west) for d in range(levs)]

    cot_east, cot_west = call(
        pack_cot_body,
        [((window, width), BF16)] * 2,
        [pltpu.VMEM((window, width), F32)] * 2,
        n_in=1,
        moved=2 * MIB,
    )(cotangent)
    cot_own_w = exchanged(cot_west, 0, west)
    cot_peer_e = exchanged(cot_east, 0, peer)
    cot_peer_w = exchanged(cot_west, 0, next_pair)

    resid, normed2 = call(
        functools.partial(window_body, levs),
        [((window, width), BF16)] * 2,
        [pltpu.VMEM((window, width), F32)],
        n_in=2 * levs + 8,
        flops=4 * 10**9,
        moved=8 * MIB,
        vmem=50,
    )(
        *easts,
        *wests,
        w_key,
        w_value,
        latent_query,
        w_agg_out,
        gain_attn[None],
        w_qkv,
        w_proj,
        gain_mlp[None],
    )
    normed2_peer = exchanged(normed2, 0, peer)
    normed2_beside = exchanged(normed2, 2, same)
    normed2_far = exchanged(normed2, 2, peer)

    out_e, out_w = call(
        mlp_body,
        [((rows, width), BF16)] * 2,
        n_in=4,
        flops=2 * 10**9,
        moved=6 * MIB,
    )(resid, normed2, w_up, w_down)
    own_rows = jnp.concatenate([out_e, exchanged(out_w, 0, east)], 0)
    beside_rows = exchanged(own_rows, 2, same)
    core_own = exchanged(own_rows, 1, same)
    core_beside = exchanged(beside_rows, 1, same)

    parity = lax.rem(lax.axis_index("tile"), 2)
    up_part = lax.dynamic_index_in_dim(
        w_up.reshape(width, groups, 2, part), parity, 2, keepdims=False
    ).reshape(width, groups * part)
    down_part = lax.dynamic_index_in_dim(
        w_down.reshape(groups, 2, part, width), parity, 1, keepdims=False
    ).reshape(groups * part, width)
    send, keep = call(
        grad_body,
        [((2 * quarter, hidden // 2), BF16), ((2 * quarter, hidden // 2), F32)],
        [pltpu.VMEM((2 * quarter, hidden // 2), F32)] * 2
        + [pltpu.VMEM((4 * window, 2 * quarter), BF16)] * 2,
        n_in=10,
        flops=5 * 10**9,
        moved=8 * MIB,
        vmem=50,
    )(
        normed2,
        normed2_beside,
        normed2_peer,
        normed2_far,
        cot_east,
        cot_own_w,
        cot_peer_e,
        cot_peer_w,
        up_part,
        down_part,
    )
    recv = exchanged(send, 1, same)
    own, *sends = call(
        functools.partial(split_body, groups),
        [((2 * quarter, part), F32)] + [((2 * quarter, part), BF16)] * (groups - 1),
        [pltpu.VMEM((groups, 2 * quarter, part), F32)],
        n_in=2,
        moved=2 * MIB,
    )(keep, recv)
    received = [
        exchanged(block, 0, lambda t, d=d: (t + 2 * d) % tiles) for d, block in enumerate(sends, 1)
    ]
    grad_up, grad_down_t = call(
        total_body,
        [((quarter, part), F32)] * 2,
        n_in=groups,
        moved=1 * MIB,
    )(own, *received)
    encoded = call(
        unpack_body,
        [((LATENT, lat, lon, width), BF16)],
        [pltpu.VMEM((window, width), F32)],
        n_in=4,
        moved=3 * MIB,
    )(own_rows, beside_rows, core_own, core_beside)[0]
    return (encoded, grad_up, grad_down_t)


def solution(mesh):
    return jax.shard_map(
        per_device,
        mesh=mesh,
        in_specs=(
            P("lev", None, "tile", None),
            P("lev"),
            P(),
            P(),
            P(),
            P(),
            P(),
            P(),
            P(),
            P(),
            P(),
            P(),
            P(None, None, "tile", None),
        ),
        out_specs=(P(None, None, "tile", None), P("lev", "tile"), P("lev", "tile")),
        check_vma=False,
    )
```

```python
import functools

import jax
import jax.numpy as jnp
from jax import lax
from jax.experimental import pallas as pl
from jax.experimental.pallas import tpu as pltpu
from jax.sharding import PartitionSpec as P

HEADS = 8
LATENT = 4
WL = 2
WA = 6
WO = 12
HALF = WO // 2
PIECE = WA * HALF
MARK = 2.0**40
F32 = jnp.float32
BF16 = jnp.bfloat16
MIB = 1 << 20


def dot(a, b, contract=((1,), (0,))):
    return lax.dot_general(a, b, (contract, ((), ())), preferred_element_type=F32)


def call(body, outs, scratch=(), vmem=40, flops=0, moved=0, n_in=1):
    return pl.pallas_call(
        body,
        out_shape=[jax.ShapeDtypeStruct(shape, dtype) for shape, dtype in outs],
        in_specs=[pl.BlockSpec(memory_space=pltpu.VMEM)] * n_in,
        out_specs=[pl.BlockSpec(memory_space=pltpu.VMEM)] * len(outs),
        scratch_shapes=list(scratch),
        compiler_params=pltpu.CompilerParams(vmem_limit_bytes=vmem * MIB),
        cost_estimate=pl.CostEstimate(flops=flops, bytes_accessed=moved, transcendentals=0),
    )


def layer_norm(rows, gain):
    mean = jnp.mean(rows, -1, keepdims=True)
    centred = rows - mean
    spread = jnp.mean(centred * centred, -1, keepdims=True)
    return (centred * lax.rsqrt(spread + 1e-05) * gain).astype(BF16)


def gelu_parts(x):
    square = x * x
    t = jnp.tanh(x * (0.7978845608028654 + 0.7978845608028654 * 0.044715 * square))
    return square, t


def lat_rolled(cells):
    return pltpu.roll(cells, cells.shape[0] - WA // 2, 0)


def pack_levels_body(lev_count, mask_ref, lev_ref, *refs):
    outs, blocks = refs[:-1], refs[-1]
    count = lev_ref.shape[0]
    me = lax.axis_index("lev")
    for j in range(count):
        live = jnp.broadcast_to(mask_ref[:, j : j + 1] > 0, lev_ref.shape[2:])
        for o in range(WO):
            cells = lat_rolled(jnp.where(live, lev_ref[j, o].astype(F32), MARK))
            half, at = 1 - o // HALF, j * PIECE + (o % HALF) * WA
            for i in range(lev_count):
                blocks[half * lev_count + i, pl.ds(at, WA)] = cells[i * WA : (i + 1) * WA]
    for half in range(2):
        for d in range(lev_count):
            outs[half * lev_count + d][...] = blocks[half * lev_count + (me ^ d)].astype(BF16)


def pack_cot_body(lev_count, cot_ref, east_ref, west_ref, blocks):
    me = lax.axis_index("lev")
    rows = LATENT * PIECE
    for l in range(LATENT):
        for o in range(WO):
            cells = lat_rolled(cot_ref[(l + WL // 2) % LATENT, o].astype(F32))
            half, at = 1 - o // HALF, l * PIECE + (o % HALF) * WA
            for i in range(lev_count):
                blocks[half * lev_count + i, pl.ds(at, WA)] = cells[i * WA : (i + 1) * WA]
    for half, ref in enumerate((east_ref, west_ref)):
        for slot in range(2):
            ref[slot * rows : (slot + 1) * rows] = blocks[
                half * lev_count + (me ^ (2 * slot))
            ].astype(BF16)


def aggregate_body(*refs):
    chunks, (query_ref, w_key, w_value, out_ref, pool) = refs[:-5], refs[-5:]
    width = w_key.shape[0]
    head_size = width // HEADS
    pairs = 2 * PIECE
    lanes = LATENT * HEADS
    owner = lax.broadcasted_iota(jnp.int32, (HEADS, width), 1) // head_size
    table = (owner == lax.broadcasted_iota(jnp.int32, (HEADS, width), 0)).astype(F32)
    query = query_ref[...].astype(F32)
    block_query = jnp.concatenate([table * query[l : l + 1] for l in range(LATENT)], 0)
    rows = jnp.concatenate([ref[...] for ref in chunks], 0)
    blocks = rows.shape[0] // pairs
    split = [slice(b * pairs, (b + 1) * pairs) for b in range(blocks)]
    keys = dot(rows, w_key[...]).astype(BF16)
    values = dot(rows, w_value[...]).astype(BF16).astype(F32)
    scores = dot(keys, block_query.astype(BF16), ((1,), (1,))) * head_size ** (-0.5)
    live = rows[:, :lanes].astype(F32) < MARK / 2
    scores = jnp.where(live, scores, -1e30)
    top = functools.reduce(jnp.maximum, [scores[at] for at in split])
    top = jnp.maximum(top, pltpu.roll(top, PIECE, 0))
    weights = [jnp.exp(scores[at] - top) * live[at].astype(F32) for at in split]
    total = functools.reduce(jnp.add, weights)
    total = total + pltpu.roll(total, PIECE, 0)
    inverse = 1.0 / total
    weights = jnp.concatenate([w * inverse for w in weights], 0)
    high = weights.astype(BF16)
    low = (weights - high.astype(F32)).astype(BF16)
    step = 256
    per = step // head_size
    for l in range(LATENT):
        slot = (l - WL // 2) % LATENT
        for n in range(width // step):
            head = lax.broadcasted_iota(jnp.int32, (lanes, step), 1) // head_size
            head = head + (l * HEADS + n * per)
            pick = (head == lax.broadcasted_iota(jnp.int32, (lanes, step), 0)).astype(BF16)
            at = slice(n * step, (n + 1) * step)
            prod = (dot(high, pick) + dot(low, pick)) * values[:, at]
            summed = functools.reduce(jnp.add, [prod[rows_at] for rows_at in split])
            summed = summed + pltpu.roll(summed, PIECE, 0)
            pool[pl.ds(slot * PIECE, PIECE), at] = summed[:PIECE]
    out_ref[...] = pool[...].astype(BF16)


def window_attention(lev_count, latent, gain, w_qkv):
    width = latent.shape[1]
    head_size = width // HEADS
    half = LATENT * PIECE
    slab = WL * PIECE
    size = 2 * slab
    normed = layer_norm(latent.astype(F32), gain[...])
    qkv = dot(normed, w_qkv[...])
    last = lax.axis_index("lev") == lev_count - 1
    shape = (2 * size, size)
    q_at = lax.rem(lax.broadcasted_iota(jnp.int32, shape, 0), slab)
    k_at = lax.rem(lax.broadcasted_iota(jnp.int32, shape, 1), slab)
    q_lat = lax.rem(q_at, WA) >= WA // 2
    k_lat = lax.rem(k_at, WA) >= WA // 2
    lat_differs = jnp.where(last, (q_lat != k_lat).astype(F32), 0.0)
    lev_differs = ((q_at >= PIECE) != (k_at >= PIECE)).astype(F32)
    lane = lax.broadcasted_iota(jnp.int32, (size, 2 * head_size), 1) < head_size
    mixed = []
    for lb in range(LATENT // WL):
        rows = jnp.concatenate(
            [qkv[lb * slab : (lb + 1) * slab], qkv[half + lb * slab : half + (lb + 1) * slab]], 0
        )
        differs = lat_differs + lev_differs if lb == LATENT // WL - 1 else lat_differs
        allowed = differs == 0.0
        outs = []
        for p in range(HEADS // 2):
            at = 2 * p * head_size
            query = rows[:, at : at + 2 * head_size]
            key = rows[:, width + at : width + at + 2 * head_size].astype(BF16)
            value = rows[:, 2 * width + at : 2 * width + at + 2 * head_size].astype(BF16)
            query = jnp.concatenate([jnp.where(lane, query, 0.0), jnp.where(lane, 0.0, query)], 0)
            scores = dot(query.astype(BF16), key, ((1,), (1,))) * head_size ** (-0.5)
            scores = jnp.where(allowed, scores, -1e30)
            weights = jnp.exp(scores - jnp.max(scores, -1, keepdims=True))
            probs = weights * (1.0 / jnp.sum(weights, -1, keepdims=True))
            out = dot(probs.astype(BF16), value)
            outs.append(jnp.where(lane, out[:size], out[size:]))
        mixed.append(jnp.concatenate(outs, 1))
    mixed = [m[:slab] for m in mixed] + [m[slab:] for m in mixed]
    return jnp.concatenate(mixed, 0).astype(BF16)


def window_body(
    lev_count,
    east,
    west,
    w_agg_out,
    gain_attn,
    w_qkv,
    w_proj,
    gain_mlp,
    resid_ref,
    normed2_ref,
):
    pooled = jnp.concatenate([east[...], west[...]], 0)
    latent = dot(pooled, w_agg_out[...]).astype(BF16)
    mixed = window_attention(lev_count, latent, gain_attn, w_qkv)
    resid = (latent.astype(F32) + dot(mixed, w_proj[...])).astype(BF16)
    resid_ref[...] = resid
    normed2_ref[...] = layer_norm(resid.astype(F32), gain_mlp[...])


def mlp_body(resid, normed2, w_up, w_down, east_ref, west_ref):
    step = 512
    rows = normed2[...]
    total = resid[...].astype(F32)
    for n in range(w_up.shape[1] // step):
        inner = dot(rows, w_up[:, n * step : (n + 1) * step])
        _, t = gelu_parts(inner)
        active = (inner * (0.5 * (1.0 + t))).astype(BF16)
        total = total + dot(active, w_down[n * step : (n + 1) * step])
    total = total.astype(BF16)
    half = rows.shape[0] // 2
    east_ref[...] = total[:half]
    west_ref[...] = total[half:]


def grad_body(chunks, last, cot_at, part, *refs):
    normed2 = refs[:chunks]
    cots = refs[chunks : chunks + 4]
    w_up, w_down = refs[chunks + 4 : chunks + 6]
    rest = refs[chunks + 6 :]
    n_half, c_half = rest[-2:]
    if last:
        sum_up, sum_dn, send, keep, acc_up, acc_dn = rest[:-2]
    else:
        acc_up, acc_dn = rest[:-2]
    me = lax.axis_index("lev")
    model, cols = acc_up.shape
    half_at = pl.ds(pl.multiple_of((me // 2) * model, model), model)
    piece = cots[0].shape[0] // 2
    rows, backs = [], []
    for k, (pair, slot) in enumerate(cot_at):
        at = slice(slot * piece, (slot + 1) * piece)
        rows.append(normed2[k][...])
        n_half[2 * k * piece : 2 * (k + 1) * piece] = normed2[k][:, half_at]
        for h in range(2):
            backs.append(cots[2 * pair + h][at])
            to = (2 * k + h) * piece
            c_half[to : to + piece] = cots[2 * pair + h][at, half_at]
    rows = jnp.concatenate(rows, 0)
    backs = jnp.concatenate(backs, 0)
    n_half_v = n_half[...]
    c_half_v = c_half[...]
    picked = w_up.shape[1] != cols
    step = part if picked else 256
    parity = lax.rem(lax.axis_index("tile"), 2)
    for n in range(cols // step):
        at = slice(n * step, (n + 1) * step)
        take = pl.ds(pl.multiple_of((2 * n + parity) * step, step), step) if picked else at
        x = dot(rows, w_up[:, take])
        back = dot(backs, w_down[take], ((1,), (1,)))
        square, t = gelu_parts(x)
        cdf = 0.5 + 0.5 * t
        active = (x * cdf).astype(BF16)
        slope = (0.5 * 0.7978845608028654) + (1.5 * 0.7978845608028654 * 0.044715) * square
        dinner = (back * (cdf + x * ((1.0 - t * t) * slope))).astype(BF16)
        up = dot(n_half_v, dinner, ((0,), (0,)))
        dn = dot(c_half_v, active, ((0,), (0,)))
        acc_up[:, at] = up + sum_up[:, at] if last else up
        acc_dn[:, at] = dn + sum_dn[:, at] if last else dn
    if last:
        quarter = model // 2
        core = lax.rem(me, 2)
        mine = pl.ds(pl.multiple_of(core * quarter, quarter), quarter)
        other = pl.ds(pl.multiple_of((1 - core) * quarter, quarter), quarter)
        keep[:quarter] = acc_up[mine]
        keep[quarter:] = acc_dn[mine]
        send[:quarter] = acc_up[other].astype(BF16)
        send[quarter:] = acc_dn[other].astype(BF16)


def split_body(groups, keep, recv, own_ref, *refs):
    outs, blocks = refs[:-1], refs[-1]
    cols = keep.shape[1] // groups
    for n in range(groups):
        at = slice(n * cols, (n + 1) * cols)
        blocks[n] = keep[:, at] + recv[:, at].astype(F32)
    me = lax.axis_index("tile") // 2
    own_ref[...] = blocks[me]
    for d in range(1, groups):
        outs[d - 1][...] = blocks[lax.rem(me + d, groups)].astype(BF16)


def total_body(own, *refs):
    received, (up_ref, dn_ref) = refs[:-2], refs[-2:]
    total = own[...]
    for part in received:
        total = total + part[...].astype(F32)
    half = total.shape[0] // 2
    up_ref[...] = total[:half]
    dn_ref[...] = total[half:]


def unpack_body(*refs):
    parts, out_ref, scratch, blocks = refs[:-3], refs[-3], refs[-2], refs[-1]
    me = lax.axis_index("lev")
    half = LATENT * PIECE
    for d, part in enumerate(parts):
        blocks[me ^ d] = part[...].astype(F32)
    for l in range(LATENT):
        for o in range(WO):
            at = (half if o < HALF else 0) + l * PIECE + (o % HALF) * WA
            cells = jnp.concatenate(
                [blocks[i, pl.ds(at, WA)] for i in range(len(parts))], 0
            )
            cells = pltpu.roll(cells, WA // 2, 0)
            out_ref[(l + WL // 2) % LATENT, o] = cells.astype(BF16)


def exchanged(block, lev_step, tile_move):
    levs, tiles = lax.axis_size("lev"), lax.axis_size("tile")
    route = [
        (l * tiles + t, (l ^ lev_step) * tiles + tile_move(t)) for l in range(levs) for t in range(tiles)
    ]
    return lax.ppermute(block, ("lev", "tile"), route)


def per_device(
    levels,
    level_mask,
    w_key,
    w_value,
    latent_query,
    w_agg_out,
    gain_attn,
    w_qkv,
    w_proj,
    gain_mlp,
    w_up,
    w_down,
    cotangent,
):
    levs, tiles = lax.axis_size("lev"), lax.axis_size("tile")
    count, lat, lon, width = levels.shape
    hidden = w_up.shape[1]
    assert lat == levs * WA and lon == WO and levs == 4 and tiles % 2 == 0
    piece = count * PIECE
    rows = LATENT * PIECE
    window = 2 * rows
    groups = tiles // 2
    part = hidden // tiles
    quarter = width // levs

    west = lambda t: (t - 1) % tiles
    east = lambda t: (t + 1) % tiles
    same = lambda t: t
    peer = lambda t: t ^ 1
    next_pair = lambda t: (t - 2) % tiles if t % 2 == 0 else t

    packed = call(
        functools.partial(pack_levels_body, levs),
        [((piece, width), BF16)] * (2 * levs),
        [pltpu.VMEM((2 * levs, piece, width), F32)],
        n_in=2,
        moved=3 * MIB,
        vmem=16,
    )(level_mask[None], levels.transpose(0, 2, 1, 3))
    easts = [packed[0]] + [exchanged(packed[d], d, same) for d in range(1, levs)]
    wests = [exchanged(packed[levs + d], d, west) for d in range(levs)]

    cot_east, cot_west = call(
        functools.partial(pack_cot_body, levs),
        [((window, width), BF16)] * 2,
        [pltpu.VMEM((2 * levs, rows, width), F32)],
        n_in=1,
        moved=2 * MIB,
        vmem=16,
    )(cotangent.transpose(0, 2, 1, 3))
    cot_own_w = exchanged(cot_west, 0, west)
    cot_peer_e = exchanged(cot_east, 0, peer)
    cot_peer_w = exchanged(cot_west, 0, next_pair)
    cots = (cot_east, cot_own_w, cot_peer_e, cot_peer_w)

    pooled = [
        call(
            aggregate_body,
            [((rows, width), BF16)],
            [pltpu.VMEM((rows, width), F32)],
            n_in=levs + 3,
            flops=10**9,
            moved=2 * MIB,
            vmem=16,
        )(*chunks, latent_query, w_key, w_value)[0]
        for chunks in (easts, wests)
    ]
    resid, normed2 = call(
        functools.partial(window_body, levs),
        [((window, width), BF16)] * 2,
        n_in=7,
        flops=2 * 10**9,
        moved=4 * MIB,
        vmem=24,
    )(*pooled, w_agg_out, gain_attn[None], w_qkv, w_proj, gain_mlp[None])
    normed2_peer = exchanged(normed2, 0, peer)
    normed2_beside = exchanged(normed2, 2, same)
    normed2_far = exchanged(normed2, 2, peer)

    out_e, out_w = call(
        mlp_body,
        [((rows, width), BF16)] * 2,
        n_in=4,
        flops=2 * 10**9,
        moved=6 * MIB,
        vmem=20,
    )(resid, normed2, w_up, w_down)
    own_rows = jnp.concatenate([out_e, exchanged(out_w, 0, east)], 0)
    all_rows = [own_rows] + [exchanged(own_rows, d, same) for d in range(1, levs)]

    if part % 128:
        parity = lax.rem(lax.axis_index("tile"), 2)
        w_up = lax.dynamic_index_in_dim(
            w_up.reshape(width, groups, 2, part), parity, 2, keepdims=False
        ).reshape(width, groups * part)
        w_down = lax.dynamic_index_in_dim(
            w_down.reshape(groups, 2, part, width), parity, 1, keepdims=False
        ).reshape(groups * part, width)
    sums = [((2 * quarter, hidden // 2), F32)] * 2
    halves = lambda n: [pltpu.VMEM((n * window, 2 * quarter), BF16)] * 2
    early = call(
        functools.partial(grad_body, 3, False, ((0, 0), (0, 1), (1, 0)), part),
        sums,
        halves(3),
        n_in=9,
        flops=4 * 10**9,
        moved=8 * MIB,
        vmem=32,
    )(normed2, normed2_beside, normed2_peer, *cots, w_up, w_down)
    send, keep = call(
        functools.partial(grad_body, 1, True, ((1, 1),), part),
        [((2 * quarter, hidden // 2), BF16), ((2 * quarter, hidden // 2), F32)],
        [pltpu.VMEM((2 * quarter, hidden // 2), F32)] * 2 + halves(1),
        n_in=9,
        flops=10**9,
        moved=8 * MIB,
        vmem=32,
    )(normed2_far, *cots, w_up, w_down, *early)
    recv = exchanged(send, 1, same)
    own, *sends = call(
        functools.partial(split_body, groups),
        [((2 * quarter, part), F32)] + [((2 * quarter, part), BF16)] * (groups - 1),
        [pltpu.VMEM((groups, 2 * quarter, part), F32)],
        n_in=2,
        moved=2 * MIB,
        vmem=32,
    )(keep, recv)
    received = [
        exchanged(block, 0, lambda t, d=d: (t + 2 * d) % tiles) for d, block in enumerate(sends, 1)
    ]
    grad_up, grad_down_t = call(
        total_body,
        [((quarter, part), F32)] * 2,
        n_in=groups,
        moved=1 * MIB,
        vmem=16,
    )(own, *received)
    encoded = call(
        unpack_body,
        [((LATENT, lon, lat, width), BF16)],
        [pltpu.VMEM((window, width), F32), pltpu.VMEM((levs, window, width), F32)],
        n_in=levs,
        moved=3 * MIB,
        vmem=24,
    )(*all_rows)[0]
    return (encoded.transpose(0, 2, 1, 3), grad_up, grad_down_t)


def solution(mesh):
    return jax.shard_map(
        per_device,
        mesh=mesh,
        in_specs=(
            P("lev", None, "tile", None),
            P("lev"),
            P(),
            P(),
            P(),
            P(),
            P(),
            P(),
            P(),
            P(),
            P(),
            P(),
            P(None, None, "tile", None),
        ),
        out_specs=(P(None, None, "tile", None), P("lev", "tile"), P("lev", "tile")),
        check_vma=False,
    )
```

```python
import functools

import jax
import jax.numpy as jnp
from jax import lax
from jax.experimental import pallas as pl
from jax.experimental.pallas import tpu as pltpu
from jax.sharding import PartitionSpec as P

HEADS = 8
LATENT = 4
WL = 2
WA = 6
WO = 12
HALF = WO // 2
PIECE = WA * HALF
MARK = 2.0**40
PIECES = ((1, 1), (0, 1), (1, 0), (0, 0))
LSE_ROWS = 16
COTS = 5
FLOPS_PER_US = 3 * 10**9
MID_US = 4.0
MLP_US = 2.0
F32 = jnp.float32
BF16 = jnp.bfloat16
MIB = 1 << 20


def dot(a, b, contract=((1,), (0,))):
    return lax.dot_general(a, b, (contract, ((), ())), preferred_element_type=F32)


def body_name(body):
    while isinstance(body, functools.partial):
        body = body.func
    return body.__name__.removesuffix("_body")


def call(body, args, outs, scratch=(), vmem=16, after=None, hbm=False, us=0.2):
    count = len(args)
    after = () if after is None else after if isinstance(after, tuple) else (after,)
    args = (*args, *after)
    name = body_name(body)
    inner = body
    if after:
        body = lambda *refs: inner(*refs[:count], *refs[count + len(after) :])
    specs = [pl.BlockSpec(memory_space=pl.ANY if hbm else pltpu.VMEM)] * count
    specs += [pl.BlockSpec(memory_space=pl.ANY)] * len(after)
    return pl.pallas_call(
        body,
        out_shape=[jax.ShapeDtypeStruct(shape, dtype) for shape, dtype in outs],
        in_specs=specs,
        out_specs=[pl.BlockSpec(memory_space=pltpu.VMEM)] * len(outs),
        scratch_shapes=list(scratch),
        compiler_params=pltpu.CompilerParams(vmem_limit_bytes=vmem * MIB),
        name=name,
        cost_estimate=pl.CostEstimate(
            flops=int(us * FLOPS_PER_US), bytes_accessed=0, transcendentals=0
        ),
    )(*args)


def layer_norm(rows, gain):
    mean = jnp.mean(rows, -1, keepdims=True)
    centred = rows - mean
    spread = jnp.mean(centred * centred, -1, keepdims=True)
    return (centred * lax.rsqrt(spread + 1e-05) * gain).astype(BF16)


def gelu_parts(x):
    square = x * x
    t = jnp.tanh(x * (0.7978845608028654 + 0.7978845608028654 * 0.044715 * square))
    return square, t


def lat_rolled(cells):
    return pltpu.roll(cells, cells.shape[0] - WA // 2, 0)


def pack_levels_body(lev_count, mask_ref, lev_ref, own_ref, send_ref, blocks):
    count = lev_ref.shape[0]
    me = lax.axis_index("lev")
    for j in range(count):
        live = jnp.broadcast_to(mask_ref[:, j : j + 1] > 0, lev_ref.shape[2:])
        for o in range(WO):
            cells = lat_rolled(jnp.where(live, lev_ref[j, o].astype(F32), MARK))
            half, at = 1 - o // HALF, j * PIECE + (o % HALF) * WA
            for i in range(lev_count):
                blocks[half * lev_count + i, pl.ds(at, WA)] = cells[i * WA : (i + 1) * WA]
    rows = count * PIECE
    for k, (half, beside) in enumerate(PIECES):
        at = slice(k * rows, (k + 1) * rows)
        mine = me ^ (2 * beside)
        own_ref[at] = blocks[half * lev_count + mine].astype(BF16)
        send_ref[at] = blocks[half * lev_count + (mine ^ 1)].astype(BF16)


def pack_cot_body(lev_count, cot_ref, east_ref, west_ref, own_east_ref, own_west_ref, blocks):
    me = lax.axis_index("lev")
    rows = LATENT * PIECE
    for l in range(LATENT):
        for o in range(WO):
            cells = lat_rolled(cot_ref[(l + WL // 2) % LATENT, o].astype(F32))
            half, at = 1 - o // HALF, l * PIECE + (o % HALF) * WA
            for i in range(lev_count):
                blocks[half * lev_count + i, pl.ds(at, WA)] = cells[i * WA : (i + 1) * WA]
    for half, (ref, own_ref) in enumerate(((east_ref, own_east_ref), (west_ref, own_west_ref))):
        for slot in range(2):
            cells = blocks[half * lev_count + (me ^ (2 * slot))].astype(BF16)
            ref[slot * rows : (slot + 1) * rows] = cells
            if slot == 0:
                own_ref[...] = cells


def head_pick(lanes, step, first):
    head = lax.broadcasted_iota(jnp.int32, (2 * lanes, step), 1) // (step // HEADS) + first
    lane = lax.broadcasted_iota(jnp.int32, (2 * lanes, step), 0) % lanes
    return (head == lane).astype(BF16)


def two_parts(value):
    high = value.astype(BF16)
    return jnp.concatenate([high, (value - high.astype(F32)).astype(BF16)], 1)


def aggregate_body(k, own, recv, query_ref, w_key, w_value, out_ref, pool):
    width = w_key.shape[0]
    head_size = width // HEADS
    pairs = 2 * PIECE
    lanes = LATENT * HEADS
    owner = lax.broadcasted_iota(jnp.int32, (HEADS, width), 1) // head_size
    table = (owner == lax.broadcasted_iota(jnp.int32, (HEADS, width), 0)).astype(F32)
    query = query_ref[...].astype(F32)
    block_query = jnp.concatenate([table * query[l : l + 1] for l in range(LATENT)], 0)
    count = own.shape[0] // len(PIECES)
    at = slice(k * count, (k + 1) * count)
    rows = jnp.concatenate([own[at], recv[at]], 0)
    blocks = rows.shape[0] // pairs
    split = [slice(b * pairs, (b + 1) * pairs) for b in range(blocks)]
    keys = dot(rows, w_key[...]).astype(BF16)
    values = dot(rows, w_value[...]).astype(BF16).astype(F32)
    scores = dot(keys, block_query.astype(BF16), ((1,), (1,))) * head_size ** (-0.5)
    live = rows[:, :lanes].astype(F32) < MARK / 2
    scores = jnp.where(live, scores, -1e30)
    top = functools.reduce(jnp.maximum, [scores[at] for at in split])
    top = jnp.maximum(top, pltpu.roll(top, PIECE, 0))
    weights = [jnp.exp(scores[at] - top) * live[at].astype(F32) for at in split]
    total = functools.reduce(jnp.add, weights)
    total = total + pltpu.roll(total, PIECE, 0)
    inverse = 1.0 / total
    both = two_parts(jnp.concatenate([w * inverse for w in weights], 0))
    for l in range(LATENT):
        slot = (l - WL // 2) % LATENT
        prod = dot(both, head_pick(lanes, width, l * HEADS)) * values
        summed = functools.reduce(jnp.add, [prod[rows_at] for rows_at in split])
        summed = summed + pltpu.roll(summed, PIECE, 0)
        pool[pl.ds(slot * PIECE, PIECE)] = summed[:PIECE]
    rows = LATENT * PIECE
    out_ref[:rows] = pool[...].astype(BF16)
    lse = top + jnp.log(total)
    high = lse.astype(BF16).astype(F32)
    middle = (lse - high).astype(BF16).astype(F32)
    parts = jnp.concatenate([high, middle, lse - high - middle, jnp.zeros_like(lse)], 1)
    parts = [parts[g * LSE_ROWS : (g + 1) * LSE_ROWS] for g in range(3)]
    parts.append(jnp.zeros_like(parts[0]))
    out_ref[rows:] = jnp.concatenate(parts, 1).astype(BF16)


def combined(first, second, pool, left, right):
    rows = LATENT * PIECE
    lanes = LATENT * HEADS
    width = first.shape[1]
    lses = []
    for ref, rows_ref in ((first, left), (second, right)):
        rows_ref[...] = ref[:rows].astype(F32)
        parts = ref[rows:].astype(F32)
        group = 4 * lanes
        parts = jnp.concatenate([parts[:, g * group : (g + 1) * group] for g in range(3)], 0)
        lses.append(parts[:, :lanes] + parts[:, lanes : 2 * lanes] + parts[:, 2 * lanes : 3 * lanes])
    share = 1.0 / (1.0 + jnp.exp(lses[1] - lses[0]))
    both = two_parts(share)
    for l in range(LATENT):
        slot = (l - WL // 2) % LATENT
        at = pl.ds(slot * PIECE, PIECE)
        spread = dot(both, head_pick(lanes, width, l * HEADS))[:PIECE]
        pool[at] = spread * left[at] + (1.0 - spread) * right[at]
    return pool[...].astype(BF16)


def combine_body(first, second, out_ref, pool, left, right):
    out_ref[...] = combined(first, second, pool, left, right)


def window_attention(lev_count, latent, gain, w_qkv):
    width = latent.shape[1]
    head_size = width // HEADS
    half = LATENT * PIECE
    slab = WL * PIECE
    size = 2 * slab
    normed = layer_norm(latent.astype(F32), gain[...])
    qkv = dot(normed, w_qkv[...])
    last = lax.axis_index("lev") == lev_count - 1
    shape = (2 * size, size)
    q_at = lax.rem(lax.broadcasted_iota(jnp.int32, shape, 0), slab)
    k_at = lax.rem(lax.broadcasted_iota(jnp.int32, shape, 1), slab)
    q_lat = lax.rem(q_at, WA) >= WA // 2
    k_lat = lax.rem(k_at, WA) >= WA // 2
    lat_differs = jnp.where(last, (q_lat != k_lat).astype(F32), 0.0)
    lev_differs = ((q_at >= PIECE) != (k_at >= PIECE)).astype(F32)
    lane = lax.broadcasted_iota(jnp.int32, (size, 2 * head_size), 1) < head_size
    mixed = []
    for lb in range(LATENT // WL):
        rows = jnp.concatenate(
            [qkv[lb * slab : (lb + 1) * slab], qkv[half + lb * slab : half + (lb + 1) * slab]], 0
        )
        differs = lat_differs + lev_differs if lb == LATENT // WL - 1 else lat_differs
        allowed = differs == 0.0
        outs = []
        for p in range(HEADS // 2):
            at = 2 * p * head_size
            query = rows[:, at : at + 2 * head_size]
            key = rows[:, width + at : width + at + 2 * head_size].astype(BF16)
            value = rows[:, 2 * width + at : 2 * width + at + 2 * head_size].astype(BF16)
            query = jnp.concatenate([jnp.where(lane, query, 0.0), jnp.where(lane, 0.0, query)], 0)
            scores = dot(query.astype(BF16), key, ((1,), (1,))) * head_size ** (-0.5)
            scores = jnp.where(allowed, scores, -1e30)
            weights = jnp.exp(scores - jnp.max(scores, -1, keepdims=True))
            probs = weights * (1.0 / jnp.sum(weights, -1, keepdims=True))
            out = dot(probs.astype(BF16), value)
            outs.append(jnp.where(lane, out[:size], out[size:]))
        mixed.append(jnp.concatenate(outs, 1))
    mixed = [m[:slab] for m in mixed] + [m[slab:] for m in mixed]
    return jnp.concatenate(mixed, 0).astype(BF16)


def window_body(
    lev_count,
    east_own,
    east_beside,
    west,
    w_agg_out,
    gain_attn,
    w_qkv,
    w_proj,
    resid_ref,
    pool,
    left,
    right,
):
    pooled = [combined(east_own, east_beside, pool, left, right), west[...]]
    latent = dot(jnp.concatenate(pooled, 0), w_agg_out[...]).astype(BF16)
    mixed = window_attention(lev_count, latent, gain_attn, w_qkv)
    resid = (latent.astype(F32) + dot(mixed, w_proj[...])).astype(BF16)
    resid_ref[...] = resid


def mlp_body(resid, gain_mlp, w_up, w_down, east_ref, west_ref):
    step = 512
    half = resid.shape[0] // 2
    total = resid[...].astype(F32)
    rows = layer_norm(total, gain_mlp[...])
    for n in range(w_up.shape[1] // step):
        inner = dot(rows, w_up[:, n * step : (n + 1) * step])
        _, t = gelu_parts(inner)
        active = (inner * (0.5 * (1.0 + t))).astype(BF16)
        total = total + dot(active, w_down[n * step : (n + 1) * step])
    total = total.astype(BF16)
    east_ref[...] = total[:half]
    west_ref[...] = total[half:]


def grad_body(chunks, cot_at, adds, last, part, *refs):
    resid = refs[:chunks]
    count = COTS if adds else 2
    cots = refs[chunks : chunks + count]
    gain, w_up, w_down = refs[chunks + count : chunks + count + 3]
    rest = refs[chunks + count + 3 :]
    normed, n_half, c_half = rest[-3:]
    if adds:
        (sum_up, sum_dn), rest = rest[:2], rest[2:]
    if last:
        (send, keep), rest = rest[:2], rest[2:]
    acc_up, acc_dn = rest[:2]
    me = lax.axis_index("lev")
    model, cols = acc_up.shape
    half_at = pl.ds(pl.multiple_of((me // 2) * model, model), model)
    piece = LATENT * PIECE
    rows = [ref[...] for ref in resid]
    backs = []
    for k, (which, slot) in enumerate(cot_at):
        at = slice(slot * piece, (slot + 1) * piece)
        to = slice(k * piece, (k + 1) * piece)
        backs.append(cots[which][at])
        c_half[to] = cots[which][at, half_at]
    rows = layer_norm(jnp.concatenate(rows, 0).astype(F32), gain[...])
    backs = jnp.concatenate(backs, 0)
    normed[...] = rows
    n_half[...] = normed[:, half_at]
    n_half_v = n_half[...]
    c_half_v = c_half[...]
    picked = w_up.shape[1] != cols
    step = part if picked else 256
    parity = lax.rem(lax.axis_index("tile"), 2)
    for n in range(cols // step):
        at = slice(n * step, (n + 1) * step)
        take = pl.ds(pl.multiple_of((2 * n + parity) * step, step), step) if picked else at
        x = dot(rows, w_up[:, take])
        back = dot(backs, w_down[take], ((1,), (1,)))
        square, t = gelu_parts(x)
        cdf = 0.5 + 0.5 * t
        active = (x * cdf).astype(BF16)
        slope = (0.5 * 0.7978845608028654) + (1.5 * 0.7978845608028654 * 0.044715) * square
        dinner = (back * (cdf + x * ((1.0 - t * t) * slope))).astype(BF16)
        up = dot(n_half_v, dinner, ((0,), (0,)))
        dn = dot(c_half_v, active, ((0,), (0,)))
        acc_up[:, at] = up + sum_up[:, at] if adds else up
        acc_dn[:, at] = dn + sum_dn[:, at] if adds else dn
    if last:
        quarter = model // 2
        core = lax.rem(me, 2)
        mine = pl.ds(pl.multiple_of(core * quarter, quarter), quarter)
        other = pl.ds(pl.multiple_of((1 - core) * quarter, quarter), quarter)
        keep[:quarter] = acc_up[mine]
        keep[quarter:] = acc_dn[mine]
        send[:quarter] = acc_up[other].astype(BF16)
        send[quarter:] = acc_dn[other].astype(BF16)


def split_body(groups, keep, recv, own_ref, *refs):
    outs, blocks = refs[:-1], refs[-1]
    cols = keep.shape[1] // groups
    for n in range(groups):
        at = slice(n * cols, (n + 1) * cols)
        blocks[n] = keep[:, at] + recv[:, at].astype(F32)
    me = lax.axis_index("tile") // 2
    own_ref[...] = blocks[me]
    for d in range(1, groups):
        outs[d - 1][...] = blocks[lax.rem(me + d, groups)].astype(BF16)


def total_body(own, *refs):
    received, (up_ref, dn_ref) = refs[:-2], refs[-2:]
    total = own[...]
    for part in received:
        total = total + part[...].astype(F32)
    half = total.shape[0] // 2
    up_ref[...] = total[:half]
    dn_ref[...] = total[half:]


def join_body(first, second, out_ref):
    half = first.shape[0]
    out_ref[:half] = first[...]
    out_ref[half:] = second[...]


def join_all_body(own_e, beside_e, west, east_ref, joined_ref):
    join_body(own_e, beside_e, east_ref)
    half = east_ref.shape[0]
    joined_ref[:half] = east_ref[...]
    joined_ref[half:] = west[...]


def hand_on_body(first, second, other, joined_ref, other_ref):
    join_body(first, second, joined_ref)
    other_ref[...] = other[...]


def unpack_body(east, west, core, out_ref, mark_ref, blocks):
    mark_ref[...] = jnp.zeros_like(mark_ref)
    me = lax.axis_index("lev")
    half = LATENT * PIECE
    for d in range(2):
        at = slice(d * half, (d + 1) * half)
        then = slice((d + 2) * half, (d + 3) * half)
        blocks[me ^ (2 * d), :half] = east[at].astype(F32)
        blocks[me ^ (2 * d), half:] = west[at].astype(F32)
        blocks[me ^ (2 * d) ^ 1, :half] = core[at].astype(F32)
        blocks[me ^ (2 * d) ^ 1, half:] = core[then].astype(F32)
    for l in range(LATENT):
        for o in range(WO):
            at = (half if o < HALF else 0) + l * PIECE + (o % HALF) * WA
            cells = jnp.concatenate(
                [blocks[i, pl.ds(at, WA)] for i in range(blocks.shape[0])], 0
            )
            cells = pltpu.roll(cells, WA // 2, 0)
            out_ref[(l + WL // 2) % LATENT, o] = cells.astype(BF16)


def exchanged(block, lev_step, tile_move):
    levs, tiles = lax.axis_size("lev"), lax.axis_size("tile")
    route = [
        (l * tiles + t, (l ^ lev_step) * tiles + tile_move(t)) for l in range(levs) for t in range(tiles)
    ]
    return lax.ppermute(block, ("lev", "tile"), route)


def per_device(
    levels,
    level_mask,
    w_key,
    w_value,
    latent_query,
    w_agg_out,
    gain_attn,
    w_qkv,
    w_proj,
    gain_mlp,
    w_up,
    w_down,
    cotangent,
):
    levs, tiles = lax.axis_size("lev"), lax.axis_size("tile")
    count, lat, lon, width = levels.shape
    hidden = w_up.shape[1]
    assert lat == levs * WA and lon == WO and levs == 4 and tiles % 2 == 0
    piece = count * PIECE
    rows = LATENT * PIECE
    window = 2 * rows
    groups = tiles // 2
    part = hidden // tiles
    quarter = width // levs

    west = lambda t: (t - 1) % tiles
    east = lambda t: (t + 1) % tiles
    same = lambda t: t
    peer = lambda t: t ^ 1
    next_pair = lambda t: (t - 2) % tiles if t % 2 == 0 else t

    cot_east, cot_west, cot_east_own, cot_west_own = call(
        functools.partial(pack_cot_body, levs),
        (cotangent.transpose(0, 2, 1, 3),),
        [((window, width), BF16)] * 2 + [((rows, width), BF16)] * 2,
        [pltpu.VMEM((2 * levs, rows, width), F32)],
        us=0.5,
    )
    cot_peer_e = exchanged(cot_east_own, 0, peer)
    cot_own_w = exchanged(cot_west_own, 0, west)
    own_raw, send_raw = call(
        functools.partial(pack_levels_body, levs),
        (level_mask[None], levels.transpose(0, 2, 1, 3)),
        [((len(PIECES) * piece, width), BF16)] * 2,
        [pltpu.VMEM((2 * levs, piece, width), F32)],
        after=cot_east,
        us=0.7,
    )
    recv_raw = exchanged(send_raw, 1, same)
    weights = (latent_query, w_key, w_value)
    aggregated = lambda k, after: call(
        functools.partial(aggregate_body, k),
        (own_raw, recv_raw, *weights),
        [((rows + LSE_ROWS, width), BF16)],
        [pltpu.VMEM((rows, width), F32)],
        after=after,
        us=1.3,
    )[0]
    pooled = [aggregated(0, None)]
    west_beside = exchanged(pooled[0], 2, same)
    pooled.append(aggregated(1, pooled[0]))
    east_beside = exchanged(pooled[1], 2, same)
    pooled.append(aggregated(2, pooled[1]))
    pooled_w = call(
        combine_body,
        (pooled[2], west_beside),
        [((rows, width), BF16)],
        [pltpu.VMEM((rows, width), F32)] * 3,
        us=0.4,
    )[0]
    pooled.append(aggregated(3, pooled_w))
    pooled_w = exchanged(pooled_w, 0, west)
    cot_joined, cot_west = call(
        hand_on_body,
        (cot_own_w, cot_peer_e, cot_west),
        [((window, width), BF16)] * 2,
        vmem=8,
        after=pooled[3],
    )
    cot_peer_w = exchanged(cot_west, 0, next_pair)
    cots = (cot_east, cot_own_w, cot_peer_e, cot_peer_w, exchanged(cot_joined, 2, same))

    resid = call(
        functools.partial(window_body, levs),
        (
            pooled[3],
            east_beside,
            pooled_w,
            w_agg_out,
            gain_attn[None],
            w_qkv,
            w_proj,
        ),
        [((window, width), BF16)],
        [pltpu.VMEM((rows, width), F32)] * 3,
        vmem=24,
        after=cot_joined,
        us=3.0,
    )[0]
    beside = exchanged(resid, 2, same)
    across = exchanged(resid, 0, peer)
    far = [exchanged(beside[:rows], 0, peer), exchanged(across[rows:], 2, same)]

    gain_mlp = gain_mlp[None]
    mlp = lambda pieces, after: call(
        mlp_body,
        (pieces, gain_mlp, w_up, w_down),
        [((rows, width), BF16)] * 2,
        vmem=20,
        after=after,
        us=MLP_US,
    )
    up_part, down_part = w_up, w_down
    if part % 128:
        parity = lax.rem(lax.axis_index("tile"), 2)
        up_part = lax.dynamic_index_in_dim(
            w_up.reshape(width, groups, 2, part), parity, 2, keepdims=False
        ).reshape(width, groups * part)
        down_part = lax.dynamic_index_in_dim(
            w_down.reshape(groups, 2, part, width), parity, 1, keepdims=False
        ).reshape(groups * part, width)
    sums = [((2 * quarter, hidden // 2), F32)] * 2
    scratch = lambda n: [pltpu.VMEM((n * rows, width), BF16)] + [
        pltpu.VMEM((n * rows, 2 * quarter), BF16)
    ] * 2
    own_at, far_at = ((0, 0), (1, 0)), ((4, 1), (3, 1))
    middle_at = ((0, 1), (4, 0), (2, 0), (3, 0))
    own_e, own_w = mlp(resid, cots[:2])
    so_far = call(
        functools.partial(grad_body, 1, own_at, False, False, part),
        (resid, *cots[:2], gain_mlp, up_part, down_part),
        sums,
        scratch(2),
        vmem=24,
        after=own_e,
        us=2.2,
    )
    beside_e, beside_w = mlp(beside, (so_far[0], *cots[3:]))
    out_w = exchanged(
        call(join_body, (own_w, beside_w), [((window, width), BF16)], vmem=8)[0], 0, east
    )
    so_far = call(
        functools.partial(grad_body, 2, middle_at, True, False, part),
        (beside, across, *cots, gain_mlp, up_part, down_part, *so_far),
        sums,
        scratch(4),
        vmem=24,
        after=beside_e,
        us=MID_US,
    )
    out_e, chip_rows = call(
        join_all_body,
        (own_e, beside_e, out_w),
        [((window, width), BF16), ((2 * window, width), BF16)],
        vmem=8,
        after=so_far[0],
    )
    send, keep = call(
        functools.partial(grad_body, 2, far_at, True, True, part),
        (*far, *cots, gain_mlp, up_part, down_part, *so_far),
        [((2 * quarter, hidden // 2), BF16), ((2 * quarter, hidden // 2), F32)],
        [pltpu.VMEM((2 * quarter, hidden // 2), F32)] * 2 + scratch(2),
        vmem=24,
        after=chip_rows,
        us=2.6,
    )
    recv = exchanged(send, 1, same)
    own, *sends = call(
        functools.partial(split_body, groups),
        (keep, recv),
        [((2 * quarter, part), F32)] + [((2 * quarter, part), BF16)] * (groups - 1),
        [pltpu.VMEM((groups, 2 * quarter, part), F32)],
        vmem=32,
    )
    received = [
        exchanged(block, 0, lambda t, d=d: (t + 2 * d) % tiles) for d, block in enumerate(sends, 1)
    ]
    core_rows = exchanged(chip_rows, 1, same)
    encoded, mark = call(
        unpack_body,
        (out_e, out_w, core_rows),
        [((LATENT, lon, lat, width), BF16), ((8, 128), F32)],
        [pltpu.VMEM((levs, window, width), F32)],
        vmem=24, us=1.6
    )
    grad_up, grad_down_t = call(
        total_body, (own, *received), [((quarter, part), F32)] * 2, after=mark, us=0.7
    )
    return (encoded.transpose(0, 2, 1, 3), grad_up, grad_down_t)


def solution(mesh):
    return jax.shard_map(
        per_device,
        mesh=mesh,
        in_specs=(
            P("lev", None, "tile", None),
            P("lev"),
            P(),
            P(),
            P(),
            P(),
            P(),
            P(),
            P(),
            P(),
            P(),
            P(),
            P(None, None, "tile", None),
        ),
        out_specs=(P(None, None, "tile", None), P("lev", "tile"), P("lev", "tile")),
        check_vma=False,
    )
```

```python
import functools

import jax
import jax.numpy as jnp
from jax import lax
from jax.experimental import pallas as pl
from jax.experimental.pallas import tpu as pltpu
from jax.sharding import PartitionSpec as P

HEADS = 8
LATENT = 4
WL = 2
WA = 6
WO = 12
HALF = WO // 2
PIECE = WA * HALF
MARK = 2.0**40
FLOPS_PER_US = 3 * 10**9
ACROSS_US = 0.05
F32 = jnp.float32
BF16 = jnp.bfloat16
MIB = 1 << 20


def dot(a, b, contract=((1,), (0,))):
    return lax.dot_general(a, b, (contract, ((), ())), preferred_element_type=F32)


def body_name(body):
    while isinstance(body, functools.partial):
        body = body.func
    return body.__name__.removesuffix("_body")


def call(body, args, outs, scratch=(), vmem=16, after=None, hbm=False, us=0.2):
    count = len(args)
    after = () if after is None else after if isinstance(after, tuple) else (after,)
    args = (*args, *after)
    name = body_name(body)
    inner = body
    if after:
        body = lambda *refs: inner(*refs[:count], *refs[count + len(after) :])
    specs = [pl.BlockSpec(memory_space=pl.ANY if hbm else pltpu.VMEM)] * count
    specs += [pl.BlockSpec(memory_space=pl.ANY)] * len(after)
    return pl.pallas_call(
        body,
        out_shape=[jax.ShapeDtypeStruct(shape, dtype) for shape, dtype in outs],
        in_specs=specs,
        out_specs=[pl.BlockSpec(memory_space=pltpu.VMEM)] * len(outs),
        scratch_shapes=list(scratch),
        compiler_params=pltpu.CompilerParams(vmem_limit_bytes=vmem * MIB),
        name=name,
        cost_estimate=pl.CostEstimate(
            flops=int(us * FLOPS_PER_US), bytes_accessed=0, transcendentals=0
        ),
    )(*args)


def layer_norm(rows, gain):
    mean = jnp.mean(rows, -1, keepdims=True)
    centred = rows - mean
    spread = jnp.mean(centred * centred, -1, keepdims=True)
    return (centred * lax.rsqrt(spread + 1e-05) * gain).astype(BF16)


def gelu_parts(x):
    square = x * x
    t = jnp.tanh(x * (0.7978845608028654 + 0.7978845608028654 * 0.044715 * square))
    return square, t


def lat_rolled(cells):
    return pltpu.roll(cells, cells.shape[0] - WA // 2, 0)


def pack_levels_body(lev_count, mask_ref, lev_ref, *refs):
    outs, core_ref, blocks = refs[:-2], refs[-2], refs[-1]
    count = lev_ref.shape[0]
    me = lax.axis_index("lev")
    for j in range(count):
        live = jnp.broadcast_to(mask_ref[:, j : j + 1] > 0, lev_ref.shape[2:])
        for o in range(WO):
            cells = lat_rolled(jnp.where(live, lev_ref[j, o].astype(F32), MARK))
            half, at = 1 - o // HALF, j * PIECE + (o % HALF) * WA
            for i in range(lev_count):
                blocks[half * lev_count + i, pl.ds(at, WA)] = cells[i * WA : (i + 1) * WA]
    rows = count * PIECE
    for half in range(2):
        for n, d in enumerate((0, 2, 3)):
            outs[3 * half + n][...] = blocks[half * lev_count + (me ^ d)].astype(BF16)
        core_ref[half * rows : (half + 1) * rows] = blocks[half * lev_count + (me ^ 1)].astype(BF16)


def pack_cot_body(lev_count, cot_ref, east_ref, west_ref, own_east_ref, own_west_ref, blocks):
    me = lax.axis_index("lev")
    rows = LATENT * PIECE
    for l in range(LATENT):
        for o in range(WO):
            cells = lat_rolled(cot_ref[(l + WL // 2) % LATENT, o].astype(F32))
            half, at = 1 - o // HALF, l * PIECE + (o % HALF) * WA
            for i in range(lev_count):
                blocks[half * lev_count + i, pl.ds(at, WA)] = cells[i * WA : (i + 1) * WA]
    for half, (ref, own_ref) in enumerate(((east_ref, own_east_ref), (west_ref, own_west_ref))):
        for slot in range(2):
            cells = blocks[half * lev_count + (me ^ (2 * slot))].astype(BF16)
            ref[slot * rows : (slot + 1) * rows] = cells
            if slot == 0:
                own_ref[...] = cells


def head_pick(lanes, step, first):
    head = lax.broadcasted_iota(jnp.int32, (2 * lanes, step), 1) // (step // HEADS) + first
    lane = lax.broadcasted_iota(jnp.int32, (2 * lanes, step), 0) % lanes
    return (head == lane).astype(BF16)


def two_parts(value):
    high = value.astype(BF16)
    return jnp.concatenate([high, (value - high.astype(F32)).astype(BF16)], 1)


def aggregate_body(half, own, beside, far, core, query_ref, w_key, w_value, out_ref, pool):
    width = w_key.shape[0]
    head_size = width // HEADS
    pairs = 2 * PIECE
    lanes = LATENT * HEADS
    owner = lax.broadcasted_iota(jnp.int32, (HEADS, width), 1) // head_size
    table = (owner == lax.broadcasted_iota(jnp.int32, (HEADS, width), 0)).astype(F32)
    query = query_ref[...].astype(F32)
    block_query = jnp.concatenate([table * query[l : l + 1] for l in range(LATENT)], 0)
    count = own.shape[0]
    rows = [own[...], beside[...], far[...], core[half * count : (half + 1) * count]]
    rows = jnp.concatenate(rows, 0)
    blocks = rows.shape[0] // pairs
    split = [slice(b * pairs, (b + 1) * pairs) for b in range(blocks)]
    keys = dot(rows, w_key[...]).astype(BF16)
    values = dot(rows, w_value[...]).astype(BF16).astype(F32)
    scores = dot(keys, block_query.astype(BF16), ((1,), (1,))) * head_size ** (-0.5)
    live = rows[:, :lanes].astype(F32) < MARK / 2
    scores = jnp.where(live, scores, -1e30)
    top = functools.reduce(jnp.maximum, [scores[at] for at in split])
    top = jnp.maximum(top, pltpu.roll(top, PIECE, 0))
    weights = [jnp.exp(scores[at] - top) * live[at].astype(F32) for at in split]
    total = functools.reduce(jnp.add, weights)
    total = total + pltpu.roll(total, PIECE, 0)
    inverse = 1.0 / total
    both = two_parts(jnp.concatenate([w * inverse for w in weights], 0))
    for l in range(LATENT):
        slot = (l - WL // 2) % LATENT
        prod = dot(both, head_pick(lanes, width, l * HEADS)) * values
        summed = functools.reduce(jnp.add, [prod[rows_at] for rows_at in split])
        summed = summed + pltpu.roll(summed, PIECE, 0)
        pool[pl.ds(slot * PIECE, PIECE)] = summed[:PIECE]
    out_ref[...] = pool[...].astype(BF16)


def window_attention(lev_count, latent, gain, w_qkv):
    width = latent.shape[1]
    head_size = width // HEADS
    half = LATENT * PIECE
    slab = WL * PIECE
    size = 2 * slab
    normed = layer_norm(latent.astype(F32), gain[...])
    qkv = dot(normed, w_qkv[...])
    last = lax.axis_index("lev") == lev_count - 1
    shape = (2 * size, size)
    q_at = lax.rem(lax.broadcasted_iota(jnp.int32, shape, 0), slab)
    k_at = lax.rem(lax.broadcasted_iota(jnp.int32, shape, 1), slab)
    q_lat = lax.rem(q_at, WA) >= WA // 2
    k_lat = lax.rem(k_at, WA) >= WA // 2
    lat_differs = jnp.where(last, (q_lat != k_lat).astype(F32), 0.0)
    lev_differs = ((q_at >= PIECE) != (k_at >= PIECE)).astype(F32)
    lane = lax.broadcasted_iota(jnp.int32, (size, 2 * head_size), 1) < head_size
    mixed = []
    for lb in range(LATENT // WL):
        rows = jnp.concatenate(
            [qkv[lb * slab : (lb + 1) * slab], qkv[half + lb * slab : half + (lb + 1) * slab]], 0
        )
        differs = lat_differs + lev_differs if lb == LATENT // WL - 1 else lat_differs
        allowed = differs == 0.0
        outs = []
        for p in range(HEADS // 2):
            at = 2 * p * head_size
            query = rows[:, at : at + 2 * head_size]
            key = rows[:, width + at : width + at + 2 * head_size].astype(BF16)
            value = rows[:, 2 * width + at : 2 * width + at + 2 * head_size].astype(BF16)
            query = jnp.concatenate([jnp.where(lane, query, 0.0), jnp.where(lane, 0.0, query)], 0)
            scores = dot(query.astype(BF16), key, ((1,), (1,))) * head_size ** (-0.5)
            scores = jnp.where(allowed, scores, -1e30)
            weights = jnp.exp(scores - jnp.max(scores, -1, keepdims=True))
            probs = weights * (1.0 / jnp.sum(weights, -1, keepdims=True))
            out = dot(probs.astype(BF16), value)
            outs.append(jnp.where(lane, out[:size], out[size:]))
        mixed.append(jnp.concatenate(outs, 1))
    mixed = [m[:slab] for m in mixed] + [m[slab:] for m in mixed]
    return jnp.concatenate(mixed, 0).astype(BF16)


def window_body(lev_count, east, west, w_agg_out, gain_attn, w_qkv, w_proj, resid_ref):
    pooled = jnp.concatenate([east[...], west[...]], 0)
    latent = dot(pooled, w_agg_out[...]).astype(BF16)
    mixed = window_attention(lev_count, latent, gain_attn, w_qkv)
    resid = (latent.astype(F32) + dot(mixed, w_proj[...])).astype(BF16)
    resid_ref[...] = resid


def mlp_body(resid, gain_mlp, w_up, w_down, east_ref, west_ref):
    step = 512
    half = resid.shape[0] // 2
    total = resid[...].astype(F32)
    rows = layer_norm(total, gain_mlp[...])
    for n in range(w_up.shape[1] // step):
        inner = dot(rows, w_up[:, n * step : (n + 1) * step])
        _, t = gelu_parts(inner)
        active = (inner * (0.5 * (1.0 + t))).astype(BF16)
        total = total + dot(active, w_down[n * step : (n + 1) * step])
    total = total.astype(BF16)
    east_ref[...] = total[:half]
    west_ref[...] = total[half:]


def grad_body(chunks, cot_at, adds, last, part, *refs):
    resid = refs[:chunks]
    count = chunks + 1 + max(which for which, _ in cot_at)
    cots = refs[chunks:count]
    gain, w_up, w_down = refs[count : count + 3]
    rest = refs[count + 3 :]
    normed, n_half, c_half = rest[-3:]
    if adds:
        (sum_up, sum_dn), rest = rest[:2], rest[2:]
    if last:
        (send, keep), rest = rest[:2], rest[2:]
    acc_up, acc_dn = rest[:2]
    me = lax.axis_index("lev")
    model, cols = acc_up.shape
    half_at = pl.ds(pl.multiple_of((me // 2) * model, model), model)
    piece = LATENT * PIECE
    rows = [ref[...] for ref in resid]
    backs = []
    for k, (which, slot) in enumerate(cot_at):
        at = slice(slot * piece, (slot + 1) * piece)
        to = slice(k * piece, (k + 1) * piece)
        backs.append(cots[which][at])
        c_half[to] = cots[which][at, half_at]
    rows = layer_norm(jnp.concatenate(rows, 0).astype(F32), gain[...])
    backs = jnp.concatenate(backs, 0)
    normed[...] = rows
    n_half[...] = normed[:, half_at]
    n_half_v = n_half[...]
    c_half_v = c_half[...]
    picked = w_up.shape[1] != cols
    step = part if picked else 256
    parity = lax.rem(lax.axis_index("tile"), 2)
    for n in range(cols // step):
        at = slice(n * step, (n + 1) * step)
        take = pl.ds(pl.multiple_of((2 * n + parity) * step, step), step) if picked else at
        x = dot(rows, w_up[:, take])
        back = dot(backs, w_down[take], ((1,), (1,)))
        square, t = gelu_parts(x)
        cdf = 0.5 + 0.5 * t
        active = (x * cdf).astype(BF16)
        slope = (0.5 * 0.7978845608028654) + (1.5 * 0.7978845608028654 * 0.044715) * square
        dinner = (back * (cdf + x * ((1.0 - t * t) * slope))).astype(BF16)
        up = dot(n_half_v, dinner, ((0,), (0,)))
        dn = dot(c_half_v, active, ((0,), (0,)))
        acc_up[:, at] = up + sum_up[:, at] if adds else up
        acc_dn[:, at] = dn + sum_dn[:, at] if adds else dn
    if last:
        quarter = model // 2
        core = lax.rem(me, 2)
        mine = pl.ds(pl.multiple_of(core * quarter, quarter), quarter)
        other = pl.ds(pl.multiple_of((1 - core) * quarter, quarter), quarter)
        keep[:quarter] = acc_up[mine]
        keep[quarter:] = acc_dn[mine]
        send[:quarter] = acc_up[other].astype(BF16)
        send[quarter:] = acc_dn[other].astype(BF16)


def split_body(groups, keep, recv, chip_rows, own_ref, rows_ref, *refs):
    outs, blocks = refs[:-1], refs[-1]
    rows_ref[...] = chip_rows[...]
    cols = keep.shape[1] // groups
    for n in range(groups):
        at = slice(n * cols, (n + 1) * cols)
        blocks[n] = keep[:, at] + recv[:, at].astype(F32)
    me = lax.axis_index("tile") // 2
    own_ref[...] = blocks[me]
    for d in range(1, groups):
        outs[d - 1][...] = blocks[me ^ d].astype(BF16)


def total_body(own, *refs):
    received, (up_ref, dn_ref) = refs[:-2], refs[-2:]
    total = own[...]
    for part in received:
        total = total + part[...].astype(F32)
    half = total.shape[0] // 2
    up_ref[...] = total[:half]
    dn_ref[...] = total[half:]


def join_body(first, second, out_ref):
    half = first.shape[0]
    out_ref[:half] = first[...]
    out_ref[half:] = second[...]


def assemble_body(*refs):
    at = 0
    for ref in refs[:-1]:
        refs[-1][at : at + ref.shape[0]] = ref[...]
        at += ref.shape[0]


def copy_body(*refs):
    half = len(refs) // 2
    for source, target in zip(refs[:half], refs[half:]):
        target[...] = source[...]


def unpack_body(own, core, out_ref, mark_ref, blocks):
    mark_ref[...] = jnp.zeros_like(mark_ref)
    me = lax.axis_index("lev")
    half = LATENT * PIECE
    for first, rows in ((me, own), (me ^ 1, core)):
        for d in range(2):
            for h in range(2):
                at = (2 * h + d) * half
                blocks[first ^ (2 * d), h * half : (h + 1) * half] = rows[at : at + half].astype(F32)
    for l in range(LATENT):
        for o in range(WO):
            at = (half if o < HALF else 0) + l * PIECE + (o % HALF) * WA
            cells = jnp.concatenate(
                [blocks[i, pl.ds(at, WA)] for i in range(blocks.shape[0])], 0
            )
            cells = pltpu.roll(cells, WA // 2, 0)
            out_ref[(l + WL // 2) % LATENT, o] = cells.astype(BF16)


def exchanged(block, lev_step, tile_move):
    levs, tiles = lax.axis_size("lev"), lax.axis_size("tile")
    route = [
        (l * tiles + t, (l ^ lev_step) * tiles + tile_move(t)) for l in range(levs) for t in range(tiles)
    ]
    return lax.ppermute(block, ("lev", "tile"), route)


def per_device(
    levels,
    level_mask,
    w_key,
    w_value,
    latent_query,
    w_agg_out,
    gain_attn,
    w_qkv,
    w_proj,
    gain_mlp,
    w_up,
    w_down,
    cotangent,
):
    levs, tiles = lax.axis_size("lev"), lax.axis_size("tile")
    count, lat, lon, width = levels.shape
    hidden = w_up.shape[1]
    assert lat == levs * WA and lon == WO and levs == 4 and tiles % 2 == 0
    piece = count * PIECE
    rows = LATENT * PIECE
    window = 2 * rows
    groups = tiles // 2
    part = hidden // tiles
    quarter = width // levs

    west = lambda t: (t - 1) % tiles
    east = lambda t: (t + 1) % tiles
    same = lambda t: t
    peer = lambda t: t ^ 1
    next_pair = lambda t: (t - 2) % tiles if t % 2 == 0 else t

    cot_east, cot_west, cot_east_own, cot_west_own = call(
        functools.partial(pack_cot_body, levs),
        (cotangent.transpose(0, 2, 1, 3),),
        [((window, width), BF16)] * 2 + [((rows, width), BF16)] * 2,
        [pltpu.VMEM((2 * levs, rows, width), F32)],
        us=0.5,
    )
    cot_peer_e = exchanged(cot_east_own, 0, peer)
    cot_own_w = exchanged(cot_west_own, 0, west)
    *pieces, core = call(
        functools.partial(pack_levels_body, levs),
        (level_mask[None], levels.transpose(0, 2, 1, 3)),
        [((piece, width), BF16)] * 6 + [((2 * piece, width), BF16)],
        [pltpu.VMEM((2 * levs, piece, width), F32)],
        after=cot_east,
        us=0.7,
    )
    core = exchanged(core, 1, same)
    pieces[1:3] = call(
        copy_body, pieces[1:3], [((piece, width), BF16)] * 2, vmem=8, after=core
    )
    east_raw, west_raw = [
        (own, exchanged(beside, 2, same), exchanged(far, 3, same), core)
        for own, beside, far in (pieces[:3], pieces[3:])
    ]
    aggregated = lambda half, chunks, after: call(
        functools.partial(aggregate_body, half),
        (*chunks, latent_query, w_key, w_value),
        [((rows, width), BF16)],
        [pltpu.VMEM((rows, width), F32)],
        after=after,
        us=2.1,
    )[0]
    west_pooled = aggregated(1, west_raw, None)
    pooled_e = aggregated(0, east_raw, west_pooled)
    pooled_w = exchanged(west_pooled, 0, west)
    cot_joined = call(
        join_body,
        (cot_own_w, cot_peer_e),
        [((window, width), BF16)],
        vmem=8,
        after=west_pooled,
    )[0]
    cot_beside = exchanged(cot_joined, 2, same)

    resid = call(
        functools.partial(window_body, levs),
        (pooled_e, pooled_w, w_agg_out, gain_attn[None], w_qkv, w_proj),
        [((window, width), BF16)],
        vmem=24,
        after=cot_joined,
        us=3.0,
    )[0]
    beside = exchanged(resid, 2, same)
    across = exchanged(resid, 0, peer)
    far = [exchanged(beside[:rows], 0, peer), exchanged(across[rows:], 2, same)]

    gain_mlp = gain_mlp[None]
    up_part, down_part = w_up, w_down
    if part % 128:
        parity = lax.rem(lax.axis_index("tile"), 2)
        up_part = lax.dynamic_index_in_dim(
            w_up.reshape(width, groups, 2, part), parity, 2, keepdims=False
        ).reshape(width, groups * part)
        down_part = lax.dynamic_index_in_dim(
            w_down.reshape(groups, 2, part, width), parity, 1, keepdims=False
        ).reshape(groups * part, width)
    sums = [((2 * quarter, hidden // 2), F32)] * 2
    scratch = lambda n: [pltpu.VMEM((n * rows, width), BF16)] + [
        pltpu.VMEM((n * rows, 2 * quarter), BF16)
    ] * 2
    mlp = lambda piece, after, us: call(
        mlp_body,
        (piece, gain_mlp, w_up, w_down),
        [((rows, width), BF16)] * 2,
        vmem=20,
        after=after,
        us=us,
    )
    weights = (gain_mlp, up_part, down_part)
    own_at, middle_at, far_at = (
        ((0, 0), (1, 0)),
        ((0, 1), (1, 0), (2, 0), (3, 0)),
        ((0, 1), (1, 1)),
    )
    so_far = call(
        functools.partial(grad_body, 1, own_at, False, False, part),
        (resid, cot_east, cot_own_w, *weights),
        sums,
        scratch(2),
        vmem=24,
        after=cot_beside,
        us=2.2,
    )
    cot_west = call(
        copy_body, (cot_west,), [((window, width), BF16)], vmem=8, after=so_far[0]
    )[0]
    cot_peer_w = exchanged(cot_west, 0, next_pair)
    own_out, own_w = mlp(resid, cot_west, 2.0)
    beside_out, beside_w = mlp(beside, (own_w, across), 3.0)
    out_w = exchanged(
        call(join_body, (own_w, beside_w), [((window, width), BF16)], vmem=8)[0], 0, east
    )
    so_far = call(
        functools.partial(grad_body, 2, middle_at, True, False, part),
        (
            *(beside, across),
            *(cot_east, cot_beside, cot_peer_e, cot_peer_w),
            *weights,
            *so_far,
        ),
        sums,
        scratch(4),
        vmem=24,
        after=beside_out,
        us=ACROSS_US,
    )
    send, keep = call(
        functools.partial(grad_body, 2, far_at, True, True, part),
        (*far, cot_beside, cot_peer_w, *weights, *so_far),
        [((2 * quarter, hidden // 2), BF16), ((2 * quarter, hidden // 2), F32)],
        [pltpu.VMEM((2 * quarter, hidden // 2), F32)] * 2 + scratch(2),
        vmem=24,
        us=2.6,
    )
    chip_rows = call(
        assemble_body,
        (own_out, beside_out, out_w),
        [((2 * window, width), BF16)],
        vmem=8,
        after=send,
        us=3.5,
    )[0]
    recv = exchanged(send, 1, same)
    own, chip_rows, *sends = call(
        functools.partial(split_body, groups),
        (keep, recv, chip_rows),
        [((2 * quarter, part), F32), ((2 * window, width), BF16)]
        + [((2 * quarter, part), BF16)] * (groups - 1),
        [pltpu.VMEM((groups, 2 * quarter, part), F32)],
        vmem=32,
    )
    received = [
        exchanged(block, 0, lambda t, d=d: t ^ (2 * d)) for d, block in enumerate(sends, 1)
    ]
    core_rows = exchanged(chip_rows, 1, same)
    encoded, mark = call(
        unpack_body,
        (chip_rows, core_rows),
        [((LATENT, lon, lat, width), BF16), ((8, 128), F32)],
        [pltpu.VMEM((levs, window, width), F32)],
        vmem=24, us=1.6
    )
    grad_up, grad_down_t = call(
        total_body, (own, *received), [((quarter, part), F32)] * 2, after=mark, us=0.7
    )
    return (encoded.transpose(0, 2, 1, 3), grad_up, grad_down_t)


def solution(mesh):
    return jax.shard_map(
        per_device,
        mesh=mesh,
        in_specs=(
            P("lev", None, "tile", None),
            P("lev"),
            P(),
            P(),
            P(),
            P(),
            P(),
            P(),
            P(),
            P(),
            P(),
            P(),
            P(None, None, "tile", None),
        ),
        out_specs=(P(None, None, "tile", None), P("lev", "tile"), P("lev", "tile")),
        check_vma=False,
    )
```

```python
import functools

import jax
import jax.numpy as jnp
from jax import lax
from jax.experimental import pallas as pl
from jax.experimental.pallas import tpu as pltpu
from jax.sharding import PartitionSpec as P

HEADS = 8
LATENT = 4
WL = 2
WA = 6
WO = 12
HALF = WO // 2
PIECE = WA * HALF
MARK = 2.0**40
FLOPS_PER_US = 3 * 10**9
ACROSS_US = 0.05
F32 = jnp.float32
BF16 = jnp.bfloat16
MIB = 1 << 20


def dot(a, b, contract=((1,), (0,))):
    return lax.dot_general(a, b, (contract, ((), ())), preferred_element_type=F32)


def body_name(body):
    while isinstance(body, functools.partial):
        body = body.func
    return body.__name__.removesuffix("_body")


def call(body, args, outs, scratch=(), vmem=16, after=None, hbm=False, us=0.2):
    count = len(args)
    after = () if after is None else after if isinstance(after, tuple) else (after,)
    args = (*args, *after)
    name = body_name(body)
    inner = body
    if after:
        body = lambda *refs: inner(*refs[:count], *refs[count + len(after) :])
    specs = [pl.BlockSpec(memory_space=pl.ANY if hbm else pltpu.VMEM)] * count
    specs += [pl.BlockSpec(memory_space=pl.ANY)] * len(after)
    return pl.pallas_call(
        body,
        out_shape=[jax.ShapeDtypeStruct(shape, dtype) for shape, dtype in outs],
        in_specs=specs,
        out_specs=[pl.BlockSpec(memory_space=pltpu.VMEM)] * len(outs),
        scratch_shapes=list(scratch),
        compiler_params=pltpu.CompilerParams(vmem_limit_bytes=vmem * MIB),
        name=name,
        cost_estimate=pl.CostEstimate(
            flops=int(us * FLOPS_PER_US), bytes_accessed=0, transcendentals=0
        ),
    )(*args)


def layer_norm(rows, gain):
    mean = jnp.mean(rows, -1, keepdims=True)
    centred = rows - mean
    spread = jnp.mean(centred * centred, -1, keepdims=True)
    return (centred * lax.rsqrt(spread + 1e-05) * gain).astype(BF16)


def gelu_parts(x):
    square = x * x
    t = jnp.tanh(x * (0.7978845608028654 + 0.7978845608028654 * 0.044715 * square))
    return square, t


def lat_rolled(cells):
    return pltpu.roll(cells, cells.shape[0] - WA // 2, 0)


def pack_levels_body(lev_count, lev_ref, *refs):
    outs, core_ref, blocks = refs[:-2], refs[-2], refs[-1]
    count = lev_ref.shape[0]
    me = lax.axis_index("lev")
    for j in range(count):
        for o in range(WO):
            cells = lat_rolled(lev_ref[j, o].astype(F32))
            half, at = 1 - o // HALF, j * PIECE + (o % HALF) * WA
            for i in range(lev_count):
                blocks[half * lev_count + i, pl.ds(at, WA)] = cells[i * WA : (i + 1) * WA]
    rows = count * PIECE
    for half in range(2):
        for n, d in enumerate((0, 2, 3)):
            outs[3 * half + n][...] = blocks[half * lev_count + (me ^ d)].astype(BF16)
        core_ref[half * rows : (half + 1) * rows] = blocks[half * lev_count + (me ^ 1)].astype(BF16)


def pack_cot_body(lev_count, cot_ref, east_ref, west_ref, own_east_ref, own_west_ref, blocks):
    me = lax.axis_index("lev")
    rows = LATENT * PIECE
    for l in range(LATENT):
        for o in range(WO):
            cells = lat_rolled(cot_ref[(l + WL // 2) % LATENT, o].astype(F32))
            half, at = 1 - o // HALF, l * PIECE + (o % HALF) * WA
            for i in range(lev_count):
                blocks[half * lev_count + i, pl.ds(at, WA)] = cells[i * WA : (i + 1) * WA]
    for half, (ref, own_ref) in enumerate(((east_ref, own_east_ref), (west_ref, own_west_ref))):
        for slot in range(2):
            cells = blocks[half * lev_count + (me ^ (2 * slot))].astype(BF16)
            ref[slot * rows : (slot + 1) * rows] = cells
            if slot == 0:
                own_ref[...] = cells


def head_pick(lanes, step, first):
    head = lax.broadcasted_iota(jnp.int32, (2 * lanes, step), 1) // (step // HEADS) + first
    lane = lax.broadcasted_iota(jnp.int32, (2 * lanes, step), 0) % lanes
    return (head == lane).astype(BF16)


def two_parts(value):
    high = value.astype(BF16)
    return jnp.concatenate([high, (value - high.astype(F32)).astype(BF16)], 1)


def aggregate_body(half, own, beside, far, core, query_ref, w_key, w_value, out_ref, pool):
    width = w_key.shape[0]
    head_size = width // HEADS
    pairs = 2 * PIECE
    lanes = LATENT * HEADS
    owner = lax.broadcasted_iota(jnp.int32, (HEADS, width), 1) // head_size
    table = (owner == lax.broadcasted_iota(jnp.int32, (HEADS, width), 0)).astype(F32)
    query = query_ref[...].astype(F32)
    block_query = jnp.concatenate([table * query[l : l + 1] for l in range(LATENT)], 0)
    count = own.shape[0]
    rows = [own[...], beside[...], far[...], core[half * count : (half + 1) * count]]
    rows = jnp.concatenate(rows, 0)
    blocks = rows.shape[0] // pairs
    split = [slice(b * pairs, (b + 1) * pairs) for b in range(blocks)]
    keys = dot(rows, w_key[...]).astype(BF16)
    values = dot(rows, w_value[...]).astype(BF16).astype(F32)
    scores = dot(keys, block_query.astype(BF16), ((1,), (1,))) * head_size ** (-0.5)
    live = rows[:, :lanes].astype(F32) < MARK / 2
    scores = jnp.where(live, scores, -1e30)
    top = functools.reduce(jnp.maximum, [scores[at] for at in split])
    top = jnp.maximum(top, pltpu.roll(top, PIECE, 0))
    weights = [jnp.exp(scores[at] - top) * live[at].astype(F32) for at in split]
    total = functools.reduce(jnp.add, weights)
    total = total + pltpu.roll(total, PIECE, 0)
    inverse = 1.0 / total
    both = two_parts(jnp.concatenate([w * inverse for w in weights], 0))
    for l in range(LATENT):
        slot = (l - WL // 2) % LATENT
        prod = dot(both, head_pick(lanes, width, l * HEADS)) * values
        summed = functools.reduce(jnp.add, [prod[rows_at] for rows_at in split])
        summed = summed + pltpu.roll(summed, PIECE, 0)
        pool[pl.ds(slot * PIECE, PIECE)] = summed[:PIECE]
    out_ref[...] = pool[...].astype(BF16)


def window_attention(lev_count, latent, gain, w_qkv):
    width = latent.shape[1]
    head_size = width // HEADS
    half = LATENT * PIECE
    slab = WL * PIECE
    size = 2 * slab
    normed = layer_norm(latent.astype(F32), gain[...])
    qkv = dot(normed, w_qkv[...])
    last = lax.axis_index("lev") == lev_count - 1
    shape = (2 * size, size)
    q_at = lax.rem(lax.broadcasted_iota(jnp.int32, shape, 0), slab)
    k_at = lax.rem(lax.broadcasted_iota(jnp.int32, shape, 1), slab)
    q_lat = lax.rem(q_at, WA) >= WA // 2
    k_lat = lax.rem(k_at, WA) >= WA // 2
    lat_differs = jnp.where(last, (q_lat != k_lat).astype(F32), 0.0)
    lev_differs = ((q_at >= PIECE) != (k_at >= PIECE)).astype(F32)
    lane = lax.broadcasted_iota(jnp.int32, (size, 2 * head_size), 1) < head_size
    mixed = []
    for lb in range(LATENT // WL):
        rows = jnp.concatenate(
            [qkv[lb * slab : (lb + 1) * slab], qkv[half + lb * slab : half + (lb + 1) * slab]], 0
        )
        differs = lat_differs + lev_differs if lb == LATENT // WL - 1 else lat_differs
        allowed = differs == 0.0
        outs = []
        for p in range(HEADS // 2):
            at = 2 * p * head_size
            query = rows[:, at : at + 2 * head_size]
            key = rows[:, width + at : width + at + 2 * head_size].astype(BF16)
            value = rows[:, 2 * width + at : 2 * width + at + 2 * head_size].astype(BF16)
            query = jnp.concatenate([jnp.where(lane, query, 0.0), jnp.where(lane, 0.0, query)], 0)
            scores = dot(query.astype(BF16), key, ((1,), (1,))) * head_size ** (-0.5)
            scores = jnp.where(allowed, scores, -1e30)
            weights = jnp.exp(scores - jnp.max(scores, -1, keepdims=True))
            probs = weights * (1.0 / jnp.sum(weights, -1, keepdims=True))
            out = dot(probs.astype(BF16), value)
            outs.append(jnp.where(lane, out[:size], out[size:]))
        mixed.append(jnp.concatenate(outs, 1))
    mixed = [m[:slab] for m in mixed] + [m[slab:] for m in mixed]
    return jnp.concatenate(mixed, 0).astype(BF16)


def window_body(lev_count, east, west, w_agg_out, gain_attn, w_qkv, w_proj, resid_ref):
    pooled = jnp.concatenate([east[...], west[...]], 0)
    latent = dot(pooled, w_agg_out[...]).astype(BF16)
    mixed = window_attention(lev_count, latent, gain_attn, w_qkv)
    resid = (latent.astype(F32) + dot(mixed, w_proj[...])).astype(BF16)
    resid_ref[...] = resid


def mlp_body(resid, gain_mlp, w_up, w_down, east_ref, west_ref):
    step = 512
    half = resid.shape[0] // 2
    total = resid[...].astype(F32)
    rows = layer_norm(total, gain_mlp[...])
    for n in range(w_up.shape[1] // step):
        inner = dot(rows, w_up[:, n * step : (n + 1) * step])
        _, t = gelu_parts(inner)
        active = (inner * (0.5 * (1.0 + t))).astype(BF16)
        total = total + dot(active, w_down[n * step : (n + 1) * step])
    total = total.astype(BF16)
    east_ref[...] = total[:half]
    west_ref[...] = total[half:]


def grad_body(chunks, cot_at, adds, last, part, *refs):
    resid = refs[:chunks]
    count = chunks + 1 + max(which for which, _ in cot_at)
    cots = refs[chunks:count]
    gain, w_up, w_down = refs[count : count + 3]
    rest = refs[count + 3 :]
    normed, n_half, c_half = rest[-3:]
    if adds:
        (sum_up, sum_dn), rest = rest[:2], rest[2:]
    if last:
        (send, keep), rest = rest[:2], rest[2:]
    acc_up, acc_dn = rest[:2]
    me = lax.axis_index("lev")
    model, cols = acc_up.shape
    half_at = pl.ds(pl.multiple_of((me // 2) * model, model), model)
    piece = LATENT * PIECE
    rows = [ref[...] for ref in resid]
    backs = []
    for k, (which, slot) in enumerate(cot_at):
        at = slice(slot * piece, (slot + 1) * piece)
        to = slice(k * piece, (k + 1) * piece)
        backs.append(cots[which][at])
        c_half[to] = cots[which][at, half_at]
    rows = layer_norm(jnp.concatenate(rows, 0).astype(F32), gain[...])
    backs = jnp.concatenate(backs, 0)
    normed[...] = rows
    n_half[...] = normed[:, half_at]
    n_half_v = n_half[...].T
    c_half_v = c_half[...].T
    picked = w_up.shape[1] != cols
    step = part if picked else 256
    parity = lax.rem(lax.axis_index("tile"), 2)
    for n in range(cols // step):
        at = slice(n * step, (n + 1) * step)
        take = pl.ds(pl.multiple_of((2 * n + parity) * step, step), step) if picked else at
        x = dot(rows, w_up[:, take])
        back = dot(backs, w_down[take], ((1,), (1,)))
        square, t = gelu_parts(x)
        cdf = 0.5 + 0.5 * t
        active = (x * cdf).astype(BF16)
        slope = (0.5 * 0.7978845608028654) + (1.5 * 0.7978845608028654 * 0.044715) * square
        dinner = (back * (cdf + x * ((1.0 - t * t) * slope))).astype(BF16)
        up = dot(n_half_v, dinner)
        dn = dot(c_half_v, active)
        acc_up[:, at] = up + sum_up[:, at] if adds else up
        acc_dn[:, at] = dn + sum_dn[:, at] if adds else dn
    if last:
        quarter = model // 2
        core = lax.rem(me, 2)
        mine = pl.ds(pl.multiple_of(core * quarter, quarter), quarter)
        other = pl.ds(pl.multiple_of((1 - core) * quarter, quarter), quarter)
        keep[:quarter] = acc_up[mine]
        keep[quarter:] = acc_dn[mine]
        send[:quarter] = acc_up[other].astype(BF16)
        send[quarter:] = acc_dn[other].astype(BF16)


def split_body(groups, keep, recv, chip_rows, own_ref, rows_ref, *refs):
    outs, blocks = refs[:-1], refs[-1]
    rows_ref[...] = chip_rows[...]
    cols = keep.shape[1] // groups
    for n in range(groups):
        at = slice(n * cols, (n + 1) * cols)
        blocks[n] = keep[:, at] + recv[:, at].astype(F32)
    me = lax.axis_index("tile") // 2
    own_ref[...] = blocks[me]
    for n, d in enumerate(range(groups - 1, 0, -1)):
        outs[n][...] = blocks[me ^ d].astype(BF16)


def total_body(own, *refs):
    received, (up_ref, dn_ref) = refs[:-2], refs[-2:]
    total = own[...]
    for part in received:
        total = total + part[...].astype(F32)
    half = total.shape[0] // 2
    up_ref[...] = total[:half]
    dn_ref[...] = total[half:]


def join_body(first, second, out_ref):
    half = first.shape[0]
    out_ref[:half] = first[...]
    out_ref[half:] = second[...]


def assemble_body(*refs):
    at = 0
    for ref in refs[:-1]:
        refs[-1][at : at + ref.shape[0]] = ref[...]
        at += ref.shape[0]


def copy_body(*refs):
    half = len(refs) // 2
    for source, target in zip(refs[:half], refs[half:]):
        target[...] = source[...]


def unpack_body(own, core, out_ref, mark_ref, blocks):
    mark_ref[...] = jnp.zeros_like(mark_ref)
    me = lax.axis_index("lev")
    half = LATENT * PIECE
    for first, rows in ((me, own), (me ^ 1, core)):
        for d in range(2):
            for h in range(2):
                at = (2 * h + d) * half
                blocks[first ^ (2 * d), h * half : (h + 1) * half] = rows[at : at + half].astype(F32)
    for l in range(LATENT):
        for o in range(WO):
            at = (half if o < HALF else 0) + l * PIECE + (o % HALF) * WA
            cells = jnp.concatenate(
                [blocks[i, pl.ds(at, WA)] for i in range(blocks.shape[0])], 0
            )
            cells = pltpu.roll(cells, WA // 2, 0)
            out_ref[(l + WL // 2) % LATENT, o] = cells.astype(BF16)


def exchanged(block, lev_step, tile_move):
    levs, tiles = lax.axis_size("lev"), lax.axis_size("tile")
    route = [
        (l * tiles + t, (l ^ lev_step) * tiles + tile_move(t)) for l in range(levs) for t in range(tiles)
    ]
    return lax.ppermute(block, ("lev", "tile"), route)


def per_device(
    levels,
    level_mask,
    w_key,
    w_value,
    latent_query,
    w_agg_out,
    gain_attn,
    w_qkv,
    w_proj,
    gain_mlp,
    w_up,
    w_down,
    cotangent,
):
    levs, tiles = lax.axis_size("lev"), lax.axis_size("tile")
    count, lat, lon, width = levels.shape
    hidden = w_up.shape[1]
    assert lat == levs * WA and lon == WO and levs == 4 and tiles % 2 == 0
    piece = count * PIECE
    rows = LATENT * PIECE
    window = 2 * rows
    groups = tiles // 2
    part = hidden // tiles
    quarter = width // levs

    west = lambda t: (t - 1) % tiles
    east = lambda t: (t + 1) % tiles
    same = lambda t: t
    peer = lambda t: t ^ 1
    next_pair = lambda t: (t - 2) % tiles if t % 2 == 0 else t

    marked = jnp.where((level_mask > 0)[:, None, None, None], levels, MARK).astype(BF16)
    marked = marked.transpose(0, 2, 1, 3)
    *pieces, core = call(
        functools.partial(pack_levels_body, levs),
        (marked,),
        [((piece, width), BF16)] * 6 + [((2 * piece, width), BF16)],
        [pltpu.VMEM((2 * levs, piece, width), F32)],
        us=0.7,
    )
    cot_east, cot_west, cot_east_own, cot_west_own = call(
        functools.partial(pack_cot_body, levs),
        (cotangent.transpose(0, 2, 1, 3),),
        [((window, width), BF16)] * 2 + [((rows, width), BF16)] * 2,
        [pltpu.VMEM((2 * levs, rows, width), F32)],
        after=pieces[0],
        us=0.5,
    )
    cot_peer_e = exchanged(cot_east_own, 0, peer)
    cot_own_w = exchanged(cot_west_own, 0, west)
    core = exchanged(core, 1, same)
    west_raw = (pieces[3], exchanged(pieces[4], 2, same), exchanged(pieces[5], 3, same), core)
    pieces[1:3] = call(
        copy_body, pieces[1:3], [((piece, width), BF16)] * 2, vmem=8, after=(core, west_raw[2])
    )
    east_raw = (pieces[0], exchanged(pieces[1], 2, same), exchanged(pieces[2], 3, same), core)
    aggregated = lambda half, chunks, after: call(
        functools.partial(aggregate_body, half),
        (*chunks, latent_query, w_key, w_value),
        [((rows, width), BF16)],
        [pltpu.VMEM((rows, width), F32)],
        after=after,
        us=2.1,
    )[0]
    west_pooled = aggregated(1, west_raw, None)
    pooled_e = aggregated(0, east_raw, west_pooled)
    pooled_w = exchanged(west_pooled, 0, west)
    cot_joined = call(
        join_body,
        (cot_own_w, cot_peer_e),
        [((window, width), BF16)],
        vmem=8,
        after=west_pooled,
    )[0]
    cot_beside = exchanged(cot_joined, 2, same)

    resid = call(
        functools.partial(window_body, levs),
        (pooled_e, pooled_w, w_agg_out, gain_attn[None], w_qkv, w_proj),
        [((window, width), BF16)],
        vmem=24,
        after=cot_joined,
        us=3.0,
    )[0]
    beside = exchanged(resid, 2, same)
    across = exchanged(resid, 0, peer)
    far = [exchanged(beside[:rows], 0, peer), exchanged(across[rows:], 2, same)]

    gain_mlp = gain_mlp[None]
    up_part, down_part = w_up, w_down
    if part % 128:
        parity = lax.rem(lax.axis_index("tile"), 2)
        up_part = lax.dynamic_index_in_dim(
            w_up.reshape(width, groups, 2, part), parity, 2, keepdims=False
        ).reshape(width, groups * part)
        down_part = lax.dynamic_index_in_dim(
            w_down.reshape(groups, 2, part, width), parity, 1, keepdims=False
        ).reshape(groups * part, width)
    sums = [((2 * quarter, hidden // 2), F32)] * 2
    scratch = lambda n: [pltpu.VMEM((n * rows, width), BF16)] + [
        pltpu.VMEM((n * rows, 2 * quarter), BF16)
    ] * 2
    mlp = lambda piece, after, us: call(
        mlp_body,
        (piece, gain_mlp, w_up, w_down),
        [((rows, width), BF16)] * 2,
        vmem=20,
        after=after,
        us=us,
    )
    weights = (gain_mlp, up_part, down_part)
    own_at, middle_at, far_at = (
        ((0, 0), (1, 0)),
        ((0, 1), (1, 0), (2, 0), (3, 0)),
        ((0, 1), (1, 1)),
    )
    so_far = call(
        functools.partial(grad_body, 1, own_at, False, False, part),
        (resid, cot_east, cot_own_w, *weights),
        sums,
        scratch(2),
        vmem=24,
        after=cot_beside,
        us=2.2,
    )
    cot_west = call(
        copy_body, (cot_west,), [((window, width), BF16)], vmem=8, after=so_far[0]
    )[0]
    cot_peer_w = exchanged(cot_west, 0, next_pair)
    own_out, own_w = mlp(resid, cot_west, 2.0)
    beside_out, beside_w = mlp(beside, (own_w, across), 3.0)
    out_w = exchanged(
        call(join_body, (own_w, beside_w), [((window, width), BF16)], vmem=8)[0], 0, east
    )
    so_far = call(
        functools.partial(grad_body, 2, middle_at, True, False, part),
        (
            *(beside, across),
            *(cot_east, cot_beside, cot_peer_e, cot_peer_w),
            *weights,
            *so_far,
        ),
        sums,
        scratch(4),
        vmem=24,
        after=beside_out,
        us=ACROSS_US,
    )
    send, keep = call(
        functools.partial(grad_body, 2, far_at, True, True, part),
        (*far, cot_beside, cot_peer_w, *weights, *so_far),
        [((2 * quarter, hidden // 2), BF16), ((2 * quarter, hidden // 2), F32)],
        [pltpu.VMEM((2 * quarter, hidden // 2), F32)] * 2 + scratch(2),
        vmem=24,
        us=2.6,
    )
    chip_rows = call(
        assemble_body,
        (own_out, beside_out, out_w),
        [((2 * window, width), BF16)],
        vmem=8,
        after=send,
        us=3.5,
    )[0]
    recv = exchanged(send, 1, same)
    own, chip_rows, *sends = call(
        functools.partial(split_body, groups),
        (keep, recv, chip_rows),
        [((2 * quarter, part), F32), ((2 * window, width), BF16)]
        + [((2 * quarter, part), BF16)] * (groups - 1),
        [pltpu.VMEM((groups, 2 * quarter, part), F32)],
        vmem=32,
    )
    received = [
        exchanged(block, 0, lambda t, d=d: t ^ (2 * d))
        for d, block in zip(range(groups - 1, 0, -1), sends)
    ]
    core_rows = exchanged(chip_rows, 1, same)
    encoded, mark = call(
        unpack_body,
        (chip_rows, core_rows),
        [((LATENT, lon, lat, width), BF16), ((8, 128), F32)],
        [pltpu.VMEM((levs, window, width), F32)],
        vmem=24, us=1.6
    )
    grad_up, grad_down_t = call(
        total_body, (own, *received), [((quarter, part), F32)] * 2, after=mark, us=0.7
    )
    return (encoded.transpose(0, 2, 1, 3), grad_up, grad_down_t)


def solution(mesh):
    return jax.shard_map(
        per_device,
        mesh=mesh,
        in_specs=(
            P("lev", None, "tile", None),
            P("lev"),
            P(),
            P(),
            P(),
            P(),
            P(),
            P(),
            P(),
            P(),
            P(),
            P(),
            P(None, None, "tile", None),
        ),
        out_specs=(P(None, None, "tile", None), P("lev", "tile"), P("lev", "tile")),
        check_vma=False,
    )
```

```python
import functools

import jax
import jax.numpy as jnp
from jax import lax
from jax.experimental import pallas as pl
from jax.experimental.pallas import tpu as pltpu
from jax.sharding import PartitionSpec as P

HEADS = 8
LATENT = 4
WL = 2
WA = 6
WO = 12
HALF = WO // 2
PIECE = WA * HALF
MARK = 2.0**40
FLOPS_PER_US = 3 * 10**9
ACROSS_US = 0.05
F32 = jnp.float32
BF16 = jnp.bfloat16
MIB = 1 << 20


def dot(a, b, contract=((1,), (0,))):
    return lax.dot_general(a, b, (contract, ((), ())), preferred_element_type=F32)


def body_name(body):
    while isinstance(body, functools.partial):
        body = body.func
    return body.__name__.removesuffix("_body")


def call(body, args, outs, scratch=(), vmem=16, after=None, hbm=False, us=0.2):
    count = len(args)
    after = () if after is None else after if isinstance(after, tuple) else (after,)
    args = (*args, *after)
    name = body_name(body)
    inner = body
    if after:
        body = lambda *refs: inner(*refs[:count], *refs[count + len(after) :])
    specs = [pl.BlockSpec(memory_space=pl.ANY if hbm else pltpu.VMEM)] * count
    specs += [pl.BlockSpec(memory_space=pl.ANY)] * len(after)
    return pl.pallas_call(
        body,
        out_shape=[jax.ShapeDtypeStruct(shape, dtype) for shape, dtype in outs],
        in_specs=specs,
        out_specs=[pl.BlockSpec(memory_space=pltpu.VMEM)] * len(outs),
        scratch_shapes=list(scratch),
        compiler_params=pltpu.CompilerParams(vmem_limit_bytes=vmem * MIB),
        name=name,
        cost_estimate=pl.CostEstimate(
            flops=int(us * FLOPS_PER_US), bytes_accessed=0, transcendentals=0
        ),
    )(*args)


def layer_norm(rows, gain):
    mean = jnp.mean(rows, -1, keepdims=True)
    centred = rows - mean
    spread = jnp.mean(centred * centred, -1, keepdims=True)
    return (centred * lax.rsqrt(spread + 1e-05) * gain).astype(BF16)


def gelu_parts(x):
    square = x * x
    t = jnp.tanh(x * (0.7978845608028654 + 0.7978845608028654 * 0.044715 * square))
    return square, t


def lat_rolled(cells):
    return pltpu.roll(cells, cells.shape[0] - WA // 2, 0)


def pack_levels_body(lev_count, lev_ref, *refs):
    outs, core_ref, blocks = refs[:-2], refs[-2], refs[-1]
    count = lev_ref.shape[0]
    me = lax.axis_index("lev")
    for j in range(count):
        for o in range(WO):
            cells = lat_rolled(lev_ref[j, o].astype(F32))
            half, at = 1 - o // HALF, j * PIECE + (o % HALF) * WA
            for i in range(lev_count):
                blocks[half * lev_count + i, pl.ds(at, WA)] = cells[i * WA : (i + 1) * WA]
    rows = count * PIECE
    for half in range(2):
        for n, d in enumerate((0, 2, 3)):
            outs[3 * half + n][...] = blocks[half * lev_count + (me ^ d)].astype(BF16)
        core_ref[half * rows : (half + 1) * rows] = blocks[half * lev_count + (me ^ 1)].astype(BF16)


def pack_cot_body(lev_count, cot_ref, east_ref, west_ref, own_east_ref, own_west_ref, blocks):
    me = lax.axis_index("lev")
    rows = LATENT * PIECE
    for l in range(LATENT):
        for o in range(WO):
            cells = lat_rolled(cot_ref[(l + WL // 2) % LATENT, o].astype(F32))
            half, at = 1 - o // HALF, l * PIECE + (o % HALF) * WA
            for i in range(lev_count):
                blocks[half * lev_count + i, pl.ds(at, WA)] = cells[i * WA : (i + 1) * WA]
    for half, (ref, own_ref) in enumerate(((east_ref, own_east_ref), (west_ref, own_west_ref))):
        for slot in range(2):
            cells = blocks[half * lev_count + (me ^ (2 * slot))].astype(BF16)
            ref[slot * rows : (slot + 1) * rows] = cells
            if slot == 0:
                own_ref[...] = cells


def head_pick(lanes, step, first):
    head = lax.broadcasted_iota(jnp.int32, (2 * lanes, step), 1) // (step // HEADS) + first
    lane = lax.broadcasted_iota(jnp.int32, (2 * lanes, step), 0) % lanes
    return (head == lane).astype(BF16)


def two_parts(value):
    high = value.astype(BF16)
    return jnp.concatenate([high, (value - high.astype(F32)).astype(BF16)], 1)


def aggregate_body(half, own, beside, far, core, query_ref, w_key, w_value, out_ref, pool):
    width = w_key.shape[0]
    head_size = width // HEADS
    pairs = 2 * PIECE
    lanes = LATENT * HEADS
    owner = lax.broadcasted_iota(jnp.int32, (HEADS, width), 1) // head_size
    table = (owner == lax.broadcasted_iota(jnp.int32, (HEADS, width), 0)).astype(F32)
    query = query_ref[...].astype(F32)
    block_query = jnp.concatenate([table * query[l : l + 1] for l in range(LATENT)], 0)
    count = own.shape[0]
    rows = [own[...], beside[...], far[...], core[half * count : (half + 1) * count]]
    rows = jnp.concatenate(rows, 0)
    blocks = rows.shape[0] // pairs
    split = [slice(b * pairs, (b + 1) * pairs) for b in range(blocks)]
    keys = dot(rows, w_key[...]).astype(BF16)
    values = dot(rows, w_value[...]).astype(BF16).astype(F32)
    scores = dot(keys, block_query.astype(BF16), ((1,), (1,))) * head_size ** (-0.5)
    live = rows[:, :lanes].astype(F32) < MARK / 2
    scores = jnp.where(live, scores, -1e30)
    top = functools.reduce(jnp.maximum, [scores[at] for at in split])
    top = jnp.maximum(top, pltpu.roll(top, PIECE, 0))
    weights = [jnp.exp(scores[at] - top) * live[at].astype(F32) for at in split]
    total = functools.reduce(jnp.add, weights)
    total = total + pltpu.roll(total, PIECE, 0)
    inverse = 1.0 / total
    both = two_parts(jnp.concatenate([w * inverse for w in weights], 0))
    for l in range(LATENT):
        slot = (l - WL // 2) % LATENT
        prod = dot(both, head_pick(lanes, width, l * HEADS)) * values
        summed = functools.reduce(jnp.add, [prod[rows_at] for rows_at in split])
        summed = summed + pltpu.roll(summed, PIECE, 0)
        pool[pl.ds(slot * PIECE, PIECE)] = summed[:PIECE]
    out_ref[...] = pool[...].astype(BF16)


def window_attention(lev_count, latent, gain, w_qkv):
    width = latent.shape[1]
    head_size = width // HEADS
    half = LATENT * PIECE
    slab = WL * PIECE
    size = 2 * slab
    normed = layer_norm(latent.astype(F32), gain[...])
    qkv = dot(normed, w_qkv[...])
    last = lax.axis_index("lev") == lev_count - 1
    shape = (2 * size, size)
    q_at = lax.rem(lax.broadcasted_iota(jnp.int32, shape, 0), slab)
    k_at = lax.rem(lax.broadcasted_iota(jnp.int32, shape, 1), slab)
    q_lat = lax.rem(q_at, WA) >= WA // 2
    k_lat = lax.rem(k_at, WA) >= WA // 2
    lat_differs = jnp.where(last, (q_lat != k_lat).astype(F32), 0.0)
    lev_differs = ((q_at >= PIECE) != (k_at >= PIECE)).astype(F32)
    lane = lax.broadcasted_iota(jnp.int32, (size, 2 * head_size), 1) < head_size
    mixed = []
    for lb in range(LATENT // WL):
        rows = jnp.concatenate(
            [qkv[lb * slab : (lb + 1) * slab], qkv[half + lb * slab : half + (lb + 1) * slab]], 0
        )
        differs = lat_differs + lev_differs if lb == LATENT // WL - 1 else lat_differs
        allowed = differs == 0.0
        outs = []
        for p in range(HEADS // 2):
            at = 2 * p * head_size
            query = rows[:, at : at + 2 * head_size]
            key = rows[:, width + at : width + at + 2 * head_size].astype(BF16)
            value = rows[:, 2 * width + at : 2 * width + at + 2 * head_size].astype(BF16)
            query = jnp.concatenate([jnp.where(lane, query, 0.0), jnp.where(lane, 0.0, query)], 0)
            scores = dot(query.astype(BF16), key, ((1,), (1,))) * head_size ** (-0.5)
            scores = jnp.where(allowed, scores, -1e30)
            weights = jnp.exp(scores - jnp.max(scores, -1, keepdims=True))
            probs = weights * (1.0 / jnp.sum(weights, -1, keepdims=True))
            out = dot(probs.astype(BF16), value)
            outs.append(jnp.where(lane, out[:size], out[size:]))
        mixed.append(jnp.concatenate(outs, 1))
    mixed = [m[:slab] for m in mixed] + [m[slab:] for m in mixed]
    return jnp.concatenate(mixed, 0).astype(BF16)


def window_body(lev_count, east, west, w_agg_out, gain_attn, w_qkv, w_proj, resid_ref):
    pooled = jnp.concatenate([east[...], west[...]], 0)
    latent = dot(pooled, w_agg_out[...]).astype(BF16)
    mixed = window_attention(lev_count, latent, gain_attn, w_qkv)
    resid = (latent.astype(F32) + dot(mixed, w_proj[...])).astype(BF16)
    resid_ref[...] = resid


def mlp_body(resid, gain_mlp, w_up, w_down, east_ref, west_ref):
    step = 512
    half = resid.shape[0] // 2
    total = resid[...].astype(F32)
    rows = layer_norm(total, gain_mlp[...])
    for n in range(w_up.shape[1] // step):
        inner = dot(rows, w_up[:, n * step : (n + 1) * step])
        _, t = gelu_parts(inner)
        active = (inner * (0.5 * (1.0 + t))).astype(BF16)
        total = total + dot(active, w_down[n * step : (n + 1) * step])
    total = total.astype(BF16)
    east_ref[...] = total[:half]
    west_ref[...] = total[half:]


def grad_body(chunks, cot_at, adds, last, part, *refs):
    resid = refs[:chunks]
    count = chunks + 1 + max(which for which, _ in cot_at)
    cots = refs[chunks:count]
    gain, w_up, w_down = refs[count : count + 3]
    rest = refs[count + 3 :]
    normed, n_half, c_half = rest[-3:]
    if adds:
        (sum_up, sum_dn), rest = rest[:2], rest[2:]
    if last:
        (send, keep), rest = rest[:2], rest[2:]
    acc_up, acc_dn = rest[:2]
    me = lax.axis_index("lev")
    model, cols = acc_up.shape
    half_at = pl.ds(pl.multiple_of((me // 2) * model, model), model)
    piece = LATENT * PIECE
    rows = [ref[...] for ref in resid]
    backs = []
    for k, (which, slot) in enumerate(cot_at):
        at = slice(slot * piece, (slot + 1) * piece)
        to = slice(k * piece, (k + 1) * piece)
        backs.append(cots[which][at])
        c_half[to] = cots[which][at, half_at]
    rows = layer_norm(jnp.concatenate(rows, 0).astype(F32), gain[...])
    backs = jnp.concatenate(backs, 0)
    normed[...] = rows
    n_half[...] = normed[:, half_at]
    n_half_v = n_half[...].T
    c_half_v = c_half[...].T
    picked = w_up.shape[1] != cols
    step = part if picked else 256
    parity = lax.rem(lax.axis_index("tile"), 2)
    for n in range(cols // step):
        at = slice(n * step, (n + 1) * step)
        take = pl.ds(pl.multiple_of((2 * n + parity) * step, step), step) if picked else at
        x = dot(rows, w_up[:, take])
        back = dot(backs, w_down[take], ((1,), (1,)))
        square, t = gelu_parts(x)
        cdf = 0.5 + 0.5 * t
        active = (x * cdf).astype(BF16)
        slope = (0.5 * 0.7978845608028654) + (1.5 * 0.7978845608028654 * 0.044715) * square
        dinner = (back * (cdf + x * ((1.0 - t * t) * slope))).astype(BF16)
        up = dot(n_half_v, dinner)
        dn = dot(c_half_v, active)
        acc_up[:, at] = up + sum_up[:, at] if adds else up
        acc_dn[:, at] = dn + sum_dn[:, at] if adds else dn
    if last:
        quarter = model // 2
        core = lax.rem(me, 2)
        mine = pl.ds(pl.multiple_of(core * quarter, quarter), quarter)
        other = pl.ds(pl.multiple_of((1 - core) * quarter, quarter), quarter)
        keep[:quarter] = acc_up[mine]
        keep[quarter:] = acc_dn[mine]
        send[:quarter] = acc_up[other].astype(BF16)
        send[quarter:] = acc_dn[other].astype(BF16)


def split_body(groups, keep, recv, chip_rows, own_ref, rows_ref, *refs):
    outs, blocks = refs[:-1], refs[-1]
    rows_ref[...] = chip_rows[...]
    cols = keep.shape[1] // groups
    for n in range(groups):
        at = slice(n * cols, (n + 1) * cols)
        blocks[n] = keep[:, at] + recv[:, at].astype(F32)
    me = lax.axis_index("tile") // 2
    own_ref[...] = blocks[me]
    for n, d in enumerate(range(groups - 1, 0, -1)):
        outs[n][...] = blocks[me ^ d].astype(BF16)


def total_body(own, *refs):
    received, (up_ref, dn_ref) = refs[:-2], refs[-2:]
    total = own[...]
    for part in received:
        total = total + part[...].astype(F32)
    half = total.shape[0] // 2
    up_ref[...] = total[:half]
    dn_ref[...] = total[half:]


def join_body(first, second, out_ref):
    half = first.shape[0]
    out_ref[:half] = first[...]
    out_ref[half:] = second[...]


def assemble_body(*refs):
    at = 0
    for ref in refs[:-1]:
        refs[-1][at : at + ref.shape[0]] = ref[...]
        at += ref.shape[0]


def copy_body(*refs):
    half = len(refs) // 2
    for source, target in zip(refs[:half], refs[half:]):
        target[...] = source[...]


def unpack_body(own, core, out_ref, mark_ref, blocks):
    mark_ref[...] = jnp.zeros_like(mark_ref)
    me = lax.axis_index("lev")
    half = LATENT * PIECE
    for first, rows in ((me, own), (me ^ 1, core)):
        for d in range(2):
            for h in range(2):
                at = (2 * h + d) * half
                blocks[first ^ (2 * d), h * half : (h + 1) * half] = rows[at : at + half].astype(F32)
    for l in range(LATENT):
        for o in range(WO):
            at = (half if o < HALF else 0) + l * PIECE + (o % HALF) * WA
            cells = jnp.concatenate(
                [blocks[i, pl.ds(at, WA)] for i in range(blocks.shape[0])], 0
            )
            cells = pltpu.roll(cells, WA // 2, 0)
            out_ref[(l + WL // 2) % LATENT, o] = cells.astype(BF16)


def exchanged(block, lev_step, tile_move):
    levs, tiles = lax.axis_size("lev"), lax.axis_size("tile")
    route = [
        (l * tiles + t, (l ^ lev_step) * tiles + tile_move(t)) for l in range(levs) for t in range(tiles)
    ]
    return lax.ppermute(block, ("lev", "tile"), route)


def per_device(
    levels,
    level_mask,
    w_key,
    w_value,
    latent_query,
    w_agg_out,
    gain_attn,
    w_qkv,
    w_proj,
    gain_mlp,
    w_up,
    w_down,
    cotangent,
):
    levs, tiles = lax.axis_size("lev"), lax.axis_size("tile")
    count, lat, lon, width = levels.shape
    hidden = w_up.shape[1]
    assert lat == levs * WA and lon == WO and levs == 4 and tiles % 2 == 0
    piece = count * PIECE
    rows = LATENT * PIECE
    window = 2 * rows
    groups = tiles // 2
    part = hidden // tiles
    quarter = width // levs

    west = lambda t: (t - 1) % tiles
    east = lambda t: (t + 1) % tiles
    same = lambda t: t
    peer = lambda t: t ^ 1
    next_pair = lambda t: (t - 2) % tiles if t % 2 == 0 else t

    marked = jnp.where((level_mask > 0)[:, None, None, None], levels, MARK).astype(BF16)
    marked = marked.transpose(0, 2, 1, 3)
    *pieces, core = call(
        functools.partial(pack_levels_body, levs),
        (marked,),
        [((piece, width), BF16)] * 6 + [((2 * piece, width), BF16)],
        [pltpu.VMEM((2 * levs, piece, width), F32)],
        us=0.7,
    )
    cot_east, cot_west, cot_east_own, cot_west_own = call(
        functools.partial(pack_cot_body, levs),
        (cotangent.transpose(0, 2, 1, 3),),
        [((window, width), BF16)] * 2 + [((rows, width), BF16)] * 2,
        [pltpu.VMEM((2 * levs, rows, width), F32)],
        after=pieces[0],
        us=0.5,
    )
    cot_peer_e = exchanged(cot_east_own, 0, peer)
    cot_own_w = exchanged(cot_west_own, 0, west)
    core = exchanged(core, 1, same)
    west_raw = (pieces[3], exchanged(pieces[4], 2, same), exchanged(pieces[5], 3, same), core)
    pieces[1:3] = call(
        copy_body, pieces[1:3], [((piece, width), BF16)] * 2, vmem=8, after=(core, west_raw[2])
    )
    east_raw = (pieces[0], exchanged(pieces[1], 2, same), exchanged(pieces[2], 3, same), core)
    aggregated = lambda half, chunks, after: call(
        functools.partial(aggregate_body, half),
        (*chunks, latent_query, w_key, w_value),
        [((rows, width), BF16)],
        [pltpu.VMEM((rows, width), F32)],
        after=after,
        us=2.1,
    )[0]
    west_pooled = aggregated(1, west_raw, None)
    pooled_e = aggregated(0, east_raw, west_pooled)
    pooled_w = exchanged(west_pooled, 0, west)
    cot_joined = call(
        join_body,
        (cot_own_w, cot_peer_e),
        [((window, width), BF16)],
        vmem=8,
        after=west_pooled,
    )[0]
    cot_beside = exchanged(cot_joined, 2, same)

    resid = call(
        functools.partial(window_body, levs),
        (pooled_e, pooled_w, w_agg_out, gain_attn[None], w_qkv, w_proj),
        [((window, width), BF16)],
        vmem=24,
        after=cot_joined,
        us=3.0,
    )[0]
    beside = exchanged(resid, 2, same)
    across = exchanged(resid, 0, peer)
    far = exchanged(across, 2, same)

    gain_mlp = gain_mlp[None]
    up_part, down_part = w_up, w_down
    if part % 128:
        parity = lax.rem(lax.axis_index("tile"), 2)
        up_part = lax.dynamic_index_in_dim(
            w_up.reshape(width, groups, 2, part), parity, 2, keepdims=False
        ).reshape(width, groups * part)
        down_part = lax.dynamic_index_in_dim(
            w_down.reshape(groups, 2, part, width), parity, 1, keepdims=False
        ).reshape(groups * part, width)
    sums = [((2 * quarter, hidden // 2), F32)] * 2
    scratch = lambda n: [pltpu.VMEM((n * rows, width), BF16)] + [
        pltpu.VMEM((n * rows, 2 * quarter), BF16)
    ] * 2
    mlp = lambda piece, after, us: call(
        mlp_body,
        (piece, gain_mlp, w_up, w_down),
        [((rows, width), BF16)] * 2,
        vmem=20,
        after=after,
        us=us,
    )
    weights = (gain_mlp, up_part, down_part)
    own_at, middle_at, far_at = (
        ((0, 0), (1, 0)),
        ((0, 1), (1, 0), (2, 0)),
        ((0, 0), (1, 1), (0, 1)),
    )
    so_far = call(
        functools.partial(grad_body, 1, own_at, False, False, part),
        (resid, cot_east, cot_own_w, *weights),
        sums,
        scratch(2),
        vmem=24,
        after=cot_beside,
        us=2.2,
    )
    cot_west = call(
        copy_body, (cot_west,), [((window, width), BF16)], vmem=8, after=so_far[0]
    )[0]
    cot_peer_w = exchanged(cot_west, 0, next_pair)
    own_out, own_w = mlp(resid, cot_west, 0.05)
    beside_out, beside_w = mlp(beside, (own_w, across), 3.0)
    out_w = exchanged(
        call(join_body, (own_w, beside_w), [((window, width), BF16)], vmem=8)[0], 0, east
    )
    so_far = call(
        functools.partial(grad_body, 2, middle_at, True, False, part),
        (
            *(beside, across[:rows]),
            *(cot_east, cot_beside, cot_peer_e),
            *weights,
            *so_far,
        ),
        sums,
        scratch(3),
        vmem=24,
        after=beside_out,
        us=ACROSS_US,
    )
    send, keep = call(
        functools.partial(grad_body, 2, far_at, True, True, part),
        (across[rows:], far, cot_peer_w, cot_beside, *weights, *so_far),
        [((2 * quarter, hidden // 2), BF16), ((2 * quarter, hidden // 2), F32)],
        [pltpu.VMEM((2 * quarter, hidden // 2), F32)] * 2 + scratch(3),
        vmem=24,
        us=2.6,
    )
    chip_rows = call(
        assemble_body,
        (own_out, beside_out, out_w),
        [((2 * window, width), BF16)],
        vmem=8,
        after=send,
        us=3.5,
    )[0]
    recv = exchanged(send, 1, same)
    own, chip_rows, *sends = call(
        functools.partial(split_body, groups),
        (keep, recv, chip_rows),
        [((2 * quarter, part), F32), ((2 * window, width), BF16)]
        + [((2 * quarter, part), BF16)] * (groups - 1),
        [pltpu.VMEM((groups, 2 * quarter, part), F32)],
        vmem=32,
    )
    received = [
        exchanged(block, 0, lambda t, d=d: t ^ (2 * d))
        for d, block in zip(range(groups - 1, 0, -1), sends)
    ]
    core_rows = exchanged(chip_rows, 1, same)
    encoded, mark = call(
        unpack_body,
        (chip_rows, core_rows),
        [((LATENT, lon, lat, width), BF16), ((8, 128), F32)],
        [pltpu.VMEM((levs, window, width), F32)],
        vmem=24, us=1.6
    )
    grad_up, grad_down_t = call(
        total_body, (own, *received), [((quarter, part), F32)] * 2, after=mark, us=0.7
    )
    return (encoded.transpose(0, 2, 1, 3), grad_up, grad_down_t)


def solution(mesh):
    return jax.shard_map(
        per_device,
        mesh=mesh,
        in_specs=(
            P("lev", None, "tile", None),
            P("lev"),
            P(),
            P(),
            P(),
            P(),
            P(),
            P(),
            P(),
            P(),
            P(),
            P(),
            P(None, None, "tile", None),
        ),
        out_specs=(P(None, None, "tile", None), P("lev", "tile"), P("lev", "tile")),
        check_vma=False,
    )
```
